32 devices in a mesh: tok: 8 (over y, x, core), ch: 4 (over z).
Axes of the slice: x: 2, y: 2, z: 4, core: 2. Of those that a mesh axis runs over, the one named last changes fastest.
Arguments:
- inputs: float32 [2048, 4096], P('tok', 'ch'), may hold values from -6 to 6
- grad_out: float32 [2048, 4096], P('tok', 'ch'), may hold values from -6 to 6
- blocks_one: float32 [8, 4, 4, 128, 128], P(None, 'ch'), may hold values from -0.1875 to 0.1875
- slots_one: int32 [8, 4, 4], P(None, 'ch'), may hold values from 0 to 512, as said below
- blocks_two: float32 [8, 4, 4, 128, 128], P(None, 'ch'), may hold values from -0.125 to 0.125
- slots_two: int32 [8, 4, 4], P(None, 'ch'), may hold values from 0 to 512, as said below
Outputs:
- grad_x: float32 [2048, 4096], P('tok', 'ch')
- grad_one: float32 [8, 4, 4, 128, 128], P('tok', 'ch')
- grad_two: float32 [8, 4, 4, 128, 128], P('tok', 'ch')
The draws below stay inside these ranges and needn't reach their ends.
Inputs may be any that keep to these rules, and one draw needn't show every extreme that they name: For each hidden shard j, the live entries of slots_one[:, j, :] (those under 512) are distinct block positions; 512 marks an empty entry, live entries stand first in each owner's list, and in every shard one owner has all 4 entries live. Likewise for slots_two: distinct live positions in each shard, 512 marks an empty entry, live entries first, one owner of each shard with all 4 entries live.
All inputs are finite; a program needn't handle non-finite values.
Results may differ from the reference program's by a relative error of at most 0.0003.
Values sent between devices are 32-bit elements; how exact they have to be, the bound alone decides.
No kernel may reach another device: no remote copies, remote signals or barrier semaphores. Data moves between devices by JAX's collectives and lax.ppermute only.
A program may use at most 192 MiB of HBM per device.

```python
import math
from functools import partial
import jax
import jax.numpy as jnp
from jax import lax

D = 4096
H = 8192
BLK = 128
CAP = 4
OWNERS = 8
SHARDS = 4
HID_DEV = 2048
SLOTS = 512
TOKENS = 2048


def owner_lists(key):

    def one_shard(shard_key):
        key_count, key_busy, key_order = jax.random.split(shard_key, 3)
        counts = jax.random.randint(key_count, (OWNERS,), 0, CAP + 1)
        busiest = jax.random.randint(key_busy, (), 0, OWNERS)
        counts = jnp.where(jnp.arange(OWNERS) == busiest, CAP, counts)
        slot_order = jax.random.permutation(key_order, SLOTS)
        starts = jnp.cumsum(counts) - counts
        places = starts[:, None] + jnp.arange(CAP)[None, :]
        is_live = jnp.arange(CAP)[None, :] < counts[:, None]
        chosen = slot_order[jnp.clip(places, 0, SLOTS - 1)]
        return jnp.where(is_live, chosen, SLOTS).astype(jnp.int32)
    shard_keys = jax.random.split(key, SHARDS)
    owner_table = jax.vmap(one_shard)(shard_keys)
    return jnp.transpose(owner_table, (1, 0, 2))


def draw_slots_one(key, part):
    return owner_lists(jax.random.fold_in(key, 11))


def draw_slots_two(key, part):
    return owner_lists(jax.random.fold_in(key, 23))


def level_of(rng, extent, shards, low, largest):
    loudness, own = 1.0, jax.random.fold_in(rng, 6)
    for axis_at, parts in shards:
        steps = jnp.exp(jax.random.uniform(jax.random.fold_in(own, axis_at), (parts,), jnp.float32, low / len(shards), largest / len(shards)))
        loudness = loudness * jnp.repeat(steps, extent[axis_at] // parts).reshape([-1 if axis == axis_at else 1 for axis in range(len(extent))])
    return loudness


def centred(own_key, extent, deviation, bound, cuts=(), kind=jnp.bfloat16):
    result = jax.random.normal(own_key, extent, jnp.float32) * deviation
    if len(cuts) > 0:
        result = level_of(own_key, extent, cuts, -0.22, 0.18) * result
    return jnp.clip(result, min=-bound, max=bound).astype(kind)


def setup_inputs(seed: int = 0) -> dict:
    key_of = jax.random.split(jax.random.key(seed), 7)
    inputs = centred(key_of[0], (TOKENS, D), 1.0, 6.0, ((0, 8), (1, 4)), jnp.float32)
    grad_out = centred(key_of[1], (TOKENS, D), 1.0, 6.0, ((0, 8), (1, 4)), jnp.float32)
    blocks_one = centred(key_of[2], (OWNERS, SHARDS, CAP, BLK, BLK), (D // 4) ** -0.5, 0.1875, ((1, 4),), jnp.float32)
    slots_one = draw_slots_one(jax.random.fold_in(key_of[6], 71), 0)
    blocks_two = centred(key_of[4], (OWNERS, SHARDS, CAP, BLK, BLK), (H // 4) ** -0.5, 0.125, ((1, 4),), jnp.float32)
    slots_two = draw_slots_two(jax.random.fold_in(key_of[6], 71), 0)
    return {"inputs": inputs, "grad_out": grad_out, "blocks_one": blocks_one, "slots_one": slots_one, "blocks_two": blocks_two, "slots_two": slots_two}


HIGH = lax.Precision.HIGHEST

def table_to_dense(block_table, first_dim, second_dim):
    block_size = block_table.shape[-1]
    grid = block_table.reshape(first_dim, second_dim, block_size, block_size).transpose(0, 2, 1, 3)
    return grid.reshape(first_dim * block_size, second_dim * block_size)

def dense_to_table(dense, first_dim, second_dim):
    block_size = dense.shape[0] // first_dim
    grid = dense.reshape(first_dim, block_size, second_dim, block_size).transpose(0, 2, 1, 3)
    return grid.reshape(first_dim * second_dim, block_size, block_size)

def rebuild(blocks, slot_ids, first_dim, second_dim):
    block_size = blocks.shape[-1]
    flat_blocks = blocks.reshape(-1, block_size, block_size)
    flat_ids = slot_ids.reshape(-1)
    empty = jnp.zeros((first_dim * second_dim, block_size, block_size), blocks.dtype)
    filled = empty.at[flat_ids].set(flat_blocks, mode='drop')
    return table_to_dense(filled, first_dim, second_dim)

def pick_blocks(block_table, slot_ids):
    return jnp.take(block_table, slot_ids, axis=0, mode='fill', fill_value=0.0)

def reference(inputs, grad_out, blocks_one, slots_one, blocks_two, slots_two):
    block_size = blocks_one.shape[-1]
    feat_blocks = D // block_size
    hid_blocks = HID_DEV // block_size
    make_one = jax.vmap(partial(rebuild, first_dim=feat_blocks, second_dim=hid_blocks), in_axes=(1, 1))
    make_two = jax.vmap(partial(rebuild, first_dim=hid_blocks, second_dim=feat_blocks), in_axes=(1, 1))
    dense_one = make_one(blocks_one, slots_one).transpose(1, 0, 2).reshape(D, H)
    dense_two = make_two(blocks_two, slots_two).reshape(H, D)
    pre_act = jnp.dot(inputs, dense_one, precision=HIGH)
    normal_cdf = 0.5 * (1.0 + lax.erf(pre_act * (1.0 / math.sqrt(2.0))))
    normal_pdf = jnp.exp(-0.5 * pre_act * pre_act) * (1.0 / math.sqrt(2.0 * math.pi))
    activated = pre_act * normal_cdf
    grad_act = jnp.dot(grad_out, dense_two.T, precision=HIGH)
    grad_pre = grad_act * (normal_cdf + pre_act * normal_pdf)
    grad_x = jnp.dot(grad_pre, dense_one.T, precision=HIGH)
    factor = 1.0 / math.sqrt(TOKENS)
    full_one = jnp.dot(inputs.T, grad_pre, precision=HIGH) * factor
    full_two = jnp.dot(activated.T, grad_out, precision=HIGH) * factor
    shard_one = full_one.reshape(D, SHARDS, HID_DEV).transpose(1, 0, 2)
    shard_two = full_two.reshape(SHARDS, HID_DEV, D)
    tables_one = jax.vmap(partial(dense_to_table, first_dim=feat_blocks, second_dim=hid_blocks))(shard_one)
    tables_two = jax.vmap(partial(dense_to_table, first_dim=hid_blocks, second_dim=feat_blocks))(shard_two)
    grad_one = jax.vmap(pick_blocks, in_axes=(0, 1), out_axes=1)(tables_one, slots_one)
    grad_two = jax.vmap(pick_blocks, in_axes=(0, 1), out_axes=1)(tables_two, slots_two)
    return (grad_x, grad_one, grad_two)
```

```python
import functools
import math

import jax
import jax.numpy as jnp
from jax import lax
from jax.experimental import pallas as pl
from jax.experimental.pallas import tpu as pltpu
from jax.sharding import PartitionSpec as P

H = 8192

VMEM_LIMIT = 26 * 2**20
HBM = pl.BlockSpec(memory_space=pl.ANY)
SMEM = pl.BlockSpec(memory_space=pltpu.SMEM)
VMEM = pl.BlockSpec(memory_space=pltpu.VMEM)
NN = (((1,), (0,)), ((), ()))
NT = (((1,), (1,)), ((), ()))
TN = (((0,), (0,)), ((), ()))

FETCH_ROWS = (
    (6, 6, 7),
    (7, 6, 8),
    (8, 7, 7),
    (7, 7, 9),
    (9, 6, 9),
    (7, 8, 7),
    (8, 8, 8),
    (7, 9, 7),
    (10, 7, 8),
    (8, 7, 11),
    (10, 8, 9),
    (8, 10, 8),
    (9, 9, 10),
    (12, 8, 12),
    (11, 11, 11),
    (16, 16, 16),
)
BACK_ROWS = (
    (5, 3, 4),
    (5, 4, 3),
    (4, 4, 5),
    (4, 5, 4),
    (5, 5, 5),
    (6, 4, 6),
    (6, 6, 6),
    (8, 8, 8),
)


def room(rows, n, most):
    bands = [min(2, 3 * (s - 1) // (n - 1)) for s in range(1, n)]
    full = max(max(row) for row in rows)
    sized = []
    for row in rows:
        caps = tuple(-(-row[b] * most // full) for b in bands)
        if caps not in sized:
            sized.append(caps)
    return sized


def split(value):
    high = value.astype(jnp.bfloat16)
    return high, (value - high.astype(jnp.float32)).astype(jnp.bfloat16)


def dot3(left, right, dims):
    left_high, left_low = split(left)
    right_high, right_low = split(right)
    dot = lambda a, b: lax.dot_general(a, b, dims, preferred_element_type=jnp.float32)
    return dot(left_high, right_high) + (dot(left_high, right_low) + dot(left_low, right_high))


def bit_of(mask, place):
    return lax.shift_right_arithmetic(mask, place) & 1


def for_bits(mask, first, count, start, visit):
    def step(k, pos):
        bit = bit_of(mask, first + k)

        @pl.when(bit == 1)
        def _():
            visit(k, pos)

        return pos + bit

    return lax.fori_loop(0, count, step, start)


def lanes(block, size):
    return pl.ds(pl.multiple_of(block * size, size), size)


META_ME, META_CORE, META_CHIP, META_MASKS = 0, 1, 2, 3


def pack_kernel(n, per_slice, meta, x, dy, *rest):
    sends, sem = rest[:-1], rest[-1]
    me = meta[META_ME]
    size = sends[0].shape[-1]

    def visit_all(act):
        for s in range(1, n):
            target = lax.rem(me + s, n)
            pos = 0
            for a, source in enumerate((x, dy)):

                def visit(k, pos, a=a, source=source, s=s):
                    act(
                        pltpu.make_async_copy(
                            source.at[:, lanes(k, size)],
                            sends[s - 1].at[pos],
                            sem.at[s - 1, a * per_slice + k],
                        )
                    )

                pos = for_bits(meta[META_MASKS + 2 * target + a], me * per_slice, per_slice, pos, visit)

    visit_all(lambda copy: copy.start())
    visit_all(lambda copy: copy.wait())


def place_kernel(n, per_slice, meta, x, dy, *rest):
    recvs, targets, sem = rest[: n - 1], rest[n - 1 : n + 1], rest[n + 1]
    me = meta[META_ME]
    size = x.shape[-1] // per_slice

    def visit_all(act):
        for s in range(n):
            first = lax.rem(me - s + n, n) * per_slice
            pos = 0
            for a, source in enumerate((x, dy)):

                def visit(k, pos, a=a, source=source, s=s, first=first):
                    block = source.at[:, lanes(k, size)] if s == 0 else recvs[s - 1].at[pos]
                    act(pltpu.make_async_copy(block, targets[a].at[first + k], sem.at[a, first + k]))

                pos = for_bits(meta[META_MASKS + 2 * me + a], first, per_slice, pos, visit)

    visit_all(lambda copy: copy.start())
    visit_all(lambda copy: copy.wait())


def load_needed(meta, sources, targets, sem, act):
    for a in (0, 1):

        def visit(k, pos, a=a):
            act(pltpu.make_async_copy(sources[a].at[k], targets[a].at[k], sem.at[a, k]))

        for_bits(meta[META_MASKS + 2 * meta[META_ME] + a], 0, targets[a].shape[0], 0, visit)


def entry_one(slots, e, feat_blocks, hid_blocks):
    s = slots[e]
    return s < feat_blocks * hid_blocks, s // hid_blocks, s % hid_blocks


def entry_two(slots, e, feat_blocks, hid_blocks):
    s = slots[e]
    return s < feat_blocks * hid_blocks, s % feat_blocks, s // feat_blocks


def active_hidden(slots_one, slots_two, feat_blocks, hid_blocks):
    def step(e, masks):
        found = []
        for mask, entry, slots in zip(masks, (entry_one, entry_two), (slots_one, slots_two)):
            live, _, h = entry(slots, e, feat_blocks, hid_blocks)
            found.append(mask | jnp.where(live, lax.shift_left(1, jnp.where(live, h, 0)), 0))
        return tuple(found)

    one, two = lax.fori_loop(0, slots_one.shape[0], step, (0, 0))
    return one & two


def need_kernel(feat_blocks, hid_blocks, slots_one, slots_two, out):
    active = active_hidden(slots_one, slots_two, feat_blocks, hid_blocks)

    def step(e, masks):
        found = []
        for mask, entry, slots in zip(masks, (entry_one, entry_two), (slots_one, slots_two)):
            live, f, h = entry(slots, e, feat_blocks, hid_blocks)
            wanted = live & (bit_of(active, jnp.where(live, h, 0)) == 1)
            found.append(mask | jnp.where(wanted, lax.shift_left(1, jnp.where(wanted, f, 0)), 0))
        return tuple(found)

    out[0], out[1] = lax.fori_loop(0, slots_one.shape[0], step, (0, 0))


def ones(mask):
    shift = lax.shift_right_logical
    pairs = mask - (shift(mask, 1) & 0x55555555)
    fours = (pairs & 0x33333333) + (shift(pairs, 2) & 0x33333333)
    eights = (fours + shift(fours, 4)) & 0x0F0F0F0F
    sixteens = eights + shift(eights, 8)
    return (sixteens + shift(sixteens, 16)) & 63


def plan_kernel(n, per_slice, fetch_rows, back_rows, where, *rest):
    masks, meta, levels = rest[:n], rest[n], rest[n + 1]
    me = where[0]
    for k in range(3):
        meta[k] = where[k]
    for s in range(n):
        place = META_MASKS + 2 * lax.rem(me - s + n, n)
        meta[place] = masks[s][0]
        meta[place + 1] = masks[s][1]
    low = (1 << per_slice) - 1
    most_fetch, most_back = [], []
    for s in range(1, n):

        def widest(i, most, s=s):
            place = META_MASKS + 2 * lax.rem(i + s, n)
            counts = [ones(lax.shift_right_logical(meta[place + a], i * per_slice) & low) for a in (0, 1)]
            return jnp.maximum(most[0], counts[0] + counts[1]), jnp.maximum(most[1], counts[0])

        fetch, back = lax.fori_loop(0, n, widest, (0, 0))
        most_fetch.append(fetch)
        most_back.insert(0, back)
    for k, (rows, most) in enumerate(((fetch_rows, most_fetch), (back_rows, most_back))):
        level = len(rows) - 1
        for r in range(len(rows) - 2, -1, -1):
            fits = most[0] <= rows[r][0]
            for s in range(1, n - 1):
                fits = fits & (most[s] <= rows[r][s])
            level = jnp.where(fits, r, level)
        levels[k] = level


def hidden_kernel(n, per_slice, hid_blocks, meta, slots_one, slots_two, x, dy, w_one, w_two, *rest):
    act_out, pre_out, own_out = rest[:3]
    backs = rest[3 : n + 2]
    xs, dys, gxs, sem, back_sem = rest[n + 2 :]
    feat_blocks = xs.shape[0]
    entries = slots_one.shape[0]
    me = meta[META_ME]
    size = xs.shape[-1]
    load = functools.partial(load_needed, meta, (x, dy), (xs, dys), sem)
    load(lambda copy: copy.start())
    active = active_hidden(slots_one, slots_two, feat_blocks, hid_blocks)
    mask_x = meta[META_MASKS + 2 * me]

    def clear_hidden(h, pos):
        act_out[h] = jnp.zeros(act_out.shape[1:], jnp.float32)
        pre_out[h] = jnp.zeros(pre_out.shape[1:], jnp.float32)

    for_bits(active, 0, hid_blocks, 0, clear_hidden)

    def clear_feature(k, pos):
        gxs[k] = jnp.zeros(gxs.shape[1:], jnp.float32)

    for_bits(mask_x, 0, feat_blocks, 0, clear_feature)
    own_out[...] = jnp.zeros(own_out.shape, jnp.float32)

    def is_active(live, h):
        return live & (bit_of(active, jnp.where(live, h, 0)) == 1)

    load(lambda copy: copy.wait())

    def forward(e, carry):
        live, f, h = entry_one(slots_one, e, feat_blocks, hid_blocks)

        @pl.when(is_active(live, h))
        def _():
            act_out[h] += dot3(xs[f], w_one[e], NN)

        live, f, h = entry_two(slots_two, e, feat_blocks, hid_blocks)

        @pl.when(is_active(live, h))
        def _():
            pre_out[h] += dot3(dys[f], w_two[e], NT)

        return carry

    lax.fori_loop(0, entries, forward, 0)

    def gelu(h, pos):
        pre_act = act_out[h]
        cdf = 0.5 * (1.0 + lax.erf(pre_act * (1.0 / math.sqrt(2.0))))
        pdf = jnp.exp(-0.5 * pre_act * pre_act) * (1.0 / math.sqrt(2.0 * math.pi))
        act_out[h] = pre_act * cdf
        pre_out[h] = pre_out[h] * (cdf + pre_act * pdf)

    for_bits(active, 0, hid_blocks, 0, gelu)

    def backward(e, carry):
        live, f, h = entry_one(slots_one, e, feat_blocks, hid_blocks)

        @pl.when(is_active(live, h))
        def _():
            gxs[f] += dot3(pre_out[h], w_one[e], NT)

        return carry

    lax.fori_loop(0, entries, backward, 0)

    def send_back(act):
        for s in range(1, n):
            first = lax.rem(me + s, n) * per_slice

            def visit(k, pos, s=s, first=first):
                act(pltpu.make_async_copy(gxs.at[first + k], backs[s - 1].at[pos], back_sem.at[first + k]))

            for_bits(mask_x, first, per_slice, 0, visit)

    send_back(lambda copy: copy.start())

    def keep(k, pos):
        own_out[:, lanes(k, size)] = gxs[me * per_slice + k]

    for_bits(mask_x, me * per_slice, per_slice, 0, keep)
    send_back(lambda copy: copy.wait())


def blocks_kernel(hid_blocks, meta, slots_one, slots_two, x, dy, act, pre, keep_out, send_out, xs, dys, sem):
    feat_blocks = xs.shape[0]
    entries = slots_one.shape[0]
    per_owner = keep_out.shape[2]
    load = functools.partial(load_needed, meta, (x, dy), (xs, dys), sem)
    load(lambda copy: copy.start())
    active = active_hidden(slots_one, slots_two, feat_blocks, hid_blocks)
    core, chip = meta[META_CORE], meta[META_CHIP]
    load(lambda copy: copy.wait())

    def step(e, carry):
        owner, c = e // per_owner, e % per_owner
        where = (owner // 2) ^ chip
        mine = (owner % 2) == core
        for w, entry, slots in ((0, entry_one, slots_one), (1, entry_two, slots_two)):
            live, f, h = entry(slots, e, feat_blocks, hid_blocks)
            wanted = live & (bit_of(active, jnp.where(live, h, 0)) == 1)
            if w == 0:
                value = lambda f=f, h=h: dot3(xs[f], pre[h], TN)
            else:
                value = lambda f=f, h=h: dot3(act[h], dys[f], TN)
            block = lax.cond(wanted, value, lambda: jnp.zeros(keep_out.shape[3:], jnp.float32))

            @pl.when(mine)
            def _():
                keep_out[where, w, c] = block

            @pl.when(jnp.logical_not(mine))
            def _():
                send_out[where, w, c] = block

        return carry

    lax.fori_loop(0, entries, step, 0)


def add_kernel(n, per_slice, meta, own, *rest):
    recvs, out, landed, sem = rest[: n - 1], rest[n - 1], rest[n], rest[n + 1]
    me = meta[META_ME]
    size = landed.shape[-1]

    def visit_all(visit):
        for s in range(1, n):
            mask = meta[META_MASKS + 2 * lax.rem(me - s + n, n)]
            for_bits(mask, me * per_slice, per_slice, 0, functools.partial(visit, s - 1))

    def copy(place, k, pos):
        return pltpu.make_async_copy(recvs[place].at[pos], landed.at[place, k], sem.at[place, k])

    visit_all(lambda place, k, pos: copy(place, k, pos).start())
    out[...] = own[...]

    def add(place, k, pos):
        copy(place, k, pos).wait()
        out[:, lanes(k, size)] += landed[place, k]

    visit_all(add)


def kernel_call(kernel, name, *, out_shape, in_specs, out_specs, scratch_shapes=(), flops=0, moved=0):
    return pl.pallas_call(
        kernel,
        out_shape=out_shape,
        in_specs=in_specs,
        out_specs=out_specs,
        scratch_shapes=scratch_shapes,
        compiler_params=pltpu.CompilerParams(vmem_limit_bytes=VMEM_LIMIT),
        cost_estimate=pl.CostEstimate(flops=flops, bytes_accessed=moved, transcendentals=0),
        name=name,
    )


def floats(*dims):
    return jax.ShapeDtypeStruct(dims, jnp.float32)


def rounds(n):
    return [[(k, (k + s) % n) for k in range(n)] for s in range(1, n)]


def fetch_blocks(caps, n, size, meta, x, dy):
    tokens, width = x.shape
    per_slice = width // size
    sends = kernel_call(
        functools.partial(pack_kernel, n, per_slice),
        "pack_blocks",
        out_shape=[floats(cap, tokens, size) for cap in caps],
        in_specs=[SMEM, HBM, HBM],
        out_specs=[HBM] * (n - 1),
        scratch_shapes=[pltpu.SemaphoreType.DMA((n - 1, 2 * per_slice))],
        moved=2 * 2**20,
    )(meta, x, dy)
    recvs = [lax.ppermute(s, "ch", move) for s, move in zip(sends, rounds(n))]
    return kernel_call(
        functools.partial(place_kernel, n, per_slice),
        "place_blocks",
        out_shape=[floats(n * per_slice, tokens, size)] * 2,
        in_specs=[SMEM, HBM, HBM] + [HBM] * (n - 1),
        out_specs=[HBM] * 2,
        scratch_shapes=[pltpu.SemaphoreType.DMA((2, n * per_slice))],
        moved=2 * 2**20,
    )(meta, x, dy, *recvs)


def send_results(caps, n, m, hid_blocks, meta, slots_one, slots_two, xs, dys, act, pre, own, *backs):
    feat_blocks, tokens, size = xs.shape
    per_slice = feat_blocks // n
    per_owner = slots_one.shape[0] // (2 * m)
    came = [lax.ppermute(b[:cap], "ch", move) for b, cap, move in zip(backs, caps, rounds(n))]
    keep, send = kernel_call(
        functools.partial(blocks_kernel, hid_blocks),
        "gradient_blocks",
        out_shape=[floats(m, 2, per_owner, size, size)] * 2,
        in_specs=[SMEM] * 3 + [HBM] * 2 + [VMEM] * 2,
        out_specs=[VMEM] * 2,
        scratch_shapes=[
            pltpu.VMEM(xs.shape, jnp.float32),
            pltpu.VMEM(xs.shape, jnp.float32),
            pltpu.SemaphoreType.DMA((2, feat_blocks)),
        ],
        flops=2 * 10**9,
        moved=16 * 2**20,
    )(meta, slots_one, slots_two, xs, dys, act, pre)
    grad_x = kernel_call(
        functools.partial(add_kernel, n, per_slice),
        "add_back",
        out_shape=floats(tokens, per_slice * size),
        in_specs=[SMEM, VMEM] + [HBM] * (n - 1),
        out_specs=VMEM,
        scratch_shapes=[
            pltpu.VMEM((n - 1, per_slice, tokens, size), jnp.float32),
            pltpu.SemaphoreType.DMA((n - 1, per_slice)),
        ],
    )(meta, own, *came)
    pairs = keep + lax.ppermute(send, "tok", [(t, t ^ 1) for t in range(2 * m)])
    total = pairs[0]
    for r in range(1, m):
        total = total + lax.ppermute(pairs[r], "tok", [(t, t ^ (2 * r)) for t in range(2 * m)])
    return grad_x, total


def body(inputs, grad_out, blocks_one, slots_one, blocks_two, slots_two):
    owners = blocks_one.shape[0]
    entries = blocks_one.shape[2]
    size = blocks_one.shape[-1]
    n, m = lax.axis_size("ch"), lax.axis_size("tok") // 2
    tokens, width = inputs.shape
    per_slice = width // size
    feat_blocks = per_slice * n
    hid_blocks = H // n // size
    ids_one, ids_two = slots_one.reshape(-1), slots_two.reshape(-1)
    w_one = blocks_one.reshape(owners * entries, size, size)
    w_two = blocks_two.reshape(owners * entries, size, size)
    ints = lambda count: jax.ShapeDtypeStruct((count,), jnp.int32)
    mine = kernel_call(
        functools.partial(need_kernel, feat_blocks, hid_blocks),
        "needed_features",
        out_shape=ints(2),
        in_specs=[SMEM] * 2,
        out_specs=SMEM,
    )(ids_one, ids_two)
    masks = [mine] + [lax.ppermute(mine, "ch", move) for move in rounds(n)]
    tok = lax.axis_index("tok")
    where = jnp.stack([lax.axis_index("ch"), tok % 2, tok // 2]).astype(jnp.int32)
    fetch_rows = room(FETCH_ROWS, n, 2 * per_slice)
    back_rows = room(BACK_ROWS, n, per_slice)
    meta, levels = kernel_call(
        functools.partial(plan_kernel, n, per_slice, fetch_rows, back_rows),
        "plan",
        out_shape=[ints(META_MASKS + 2 * n), ints(2)],
        in_specs=[SMEM] * (n + 1),
        out_specs=[SMEM] * 2,
    )(where, *masks)
    xs, dys = lax.switch(
        levels[0], [functools.partial(fetch_blocks, row, n, size) for row in fetch_rows], meta, inputs, grad_out
    )
    act, pre, own, *backs = kernel_call(
        functools.partial(hidden_kernel, n, per_slice, hid_blocks),
        "hidden_blocks",
        out_shape=[
            floats(hid_blocks, tokens, size),
            floats(hid_blocks, tokens, size),
            floats(tokens, width),
            *[floats(per_slice, tokens, size)] * (n - 1),
        ],
        in_specs=[SMEM] * 3 + [HBM] * 2 + [VMEM] * 2,
        out_specs=[VMEM] * 3 + [HBM] * (n - 1),
        scratch_shapes=[
            pltpu.VMEM((feat_blocks, tokens, size), jnp.float32),
            pltpu.VMEM((feat_blocks, tokens, size), jnp.float32),
            pltpu.VMEM((feat_blocks, tokens, size), jnp.float32),
            pltpu.SemaphoreType.DMA((2, feat_blocks)),
            pltpu.SemaphoreType.DMA((feat_blocks,)),
        ],
        flops=3 * 10**9,
        moved=16 * 2**20,
    )(meta, ids_one, ids_two, xs, dys, w_one, w_two)
    grad_x, total = lax.switch(
        levels[1],
        [functools.partial(send_results, row, n, m, hid_blocks) for row in back_rows],
        meta,
        ids_one,
        ids_two,
        xs,
        dys,
        act,
        pre,
        own,
        *backs,
    )
    factor = 1.0 / math.sqrt(inputs.shape[0] * lax.axis_size("tok"))
    scaled = total * factor
    grad_one = scaled[0].reshape(1, 1, entries, size, size)
    grad_two = scaled[1].reshape(1, 1, entries, size, size)
    return (grad_x, grad_one, grad_two)


def solution(mesh):
    in_specs = (
        P("tok", "ch"),
        P("tok", "ch"),
        P(None, "ch", None, None, None),
        P(None, "ch", None),
        P(None, "ch", None, None, None),
        P(None, "ch", None),
    )
    out_specs = (P("tok", "ch"), P("tok", "ch", None, None, None), P("tok", "ch", None, None, None))
    return jax.shard_map(body, mesh=mesh, in_specs=in_specs, out_specs=out_specs, check_vma=False)
```

```python
import functools
import math

import jax
import jax.numpy as jnp
from jax import lax
from jax.experimental import pallas as pl
from jax.experimental.pallas import tpu as pltpu
from jax.sharding import PartitionSpec as P

H = 8192

VMEM_LIMIT = 36 * 2**20
ANY = pl.BlockSpec(memory_space=pl.ANY)
SMEM = pl.BlockSpec(memory_space=pltpu.SMEM)
VMEM = pl.BlockSpec(memory_space=pltpu.VMEM)
NN = (((1,), (0,)), ((), ()))
NT = (((1,), (1,)), ((), ()))
TN = (((0,), (0,)), ((), ()))

FETCH_ROWS = (
    (10, 6, 6),
    (11, 7, 6),
    (11, 6, 7),
    (12, 7, 7),
    (12, 8, 6),
    (13, 7, 8),
    (13, 6, 9),
    (14, 9, 7),
    (14, 8, 8),
    (15, 7, 10),
    (15, 10, 7),
    (16, 9, 9),
    (16, 8, 12),
    (16, 12, 8),
    (16, 11, 11),
    (16, 16, 16),
)
BACK_ROWS = (
    (6, 3, 4),
    (6, 4, 3),
    (7, 4, 4),
    (8, 4, 5),
    (8, 5, 4),
    (8, 5, 6),
    (8, 6, 5),
    (8, 8, 8),
)


def room(rows, n, most):
    bands = [0 if r < n // 2 else 1 + r % 2 for r in range(1, n)]
    full = max(max(row) for row in rows)
    sized = []
    for row in rows:
        caps = tuple(-(-row[b] * most // full) for b in bands)
        if caps not in sized:
            sized.append(caps)
    return sized


def split(value):
    high = value.astype(jnp.bfloat16)
    return high, (value - high.astype(jnp.float32)).astype(jnp.bfloat16)


def halves(value):
    return jnp.concatenate(split(value), axis=1)


def dot_wide(left, right, dims):
    return lax.dot_general(left, right, dims, preferred_element_type=jnp.float32)


def dot_nn(left, right):
    high, low = split(right)
    both = jnp.concatenate(
        [
            jnp.concatenate([high, low], axis=1),
            jnp.concatenate([high, jnp.zeros_like(low)], axis=1),
        ],
        axis=0,
    )
    out = dot_wide(halves(left), both, NN)
    size = right.shape[1]
    return out[:, :size] + out[:, size:]


def dot_nt(left, right):
    high, low = split(right)
    both = jnp.concatenate(
        [
            jnp.concatenate([high, high], axis=1),
            jnp.concatenate([low, jnp.zeros_like(low)], axis=1),
        ],
        axis=0,
    )
    out = dot_wide(halves(left), both, NT)
    size = right.shape[0]
    return out[:, :size] + out[:, size:]


def dot_tn(left, right):
    out = dot_wide(halves(left), halves(right), TN)
    rows, columns = left.shape[1], right.shape[1]
    return out[:rows, :columns] + (out[:rows, columns:] + out[rows:, :columns])


def bit_of(mask, place):
    return lax.shift_right_arithmetic(mask, place) & 1


def for_bits(mask, first, count, start, visit):
    def step(k, pos):
        bit = bit_of(mask, first + k)

        @pl.when(bit == 1)
        def _():
            visit(k, pos)

        return pos + bit

    return lax.fori_loop(0, count, step, start)


def lanes(block, size):
    return pl.ds(pl.multiple_of(block * size, size), size)


GROUP = 4
UNROLL = 8
META_ME, META_CORE, META_CHIP, META_MASKS = 0, 1, 2, 3


def pack_kernel(n, per_slice, meta, x, dy, *rest):
    sends, sem = rest[:-1], rest[-1]
    me = meta[META_ME]
    size = sends[0].shape[-1]

    def visit_all(act):
        for s in range(1, n):
            target = me ^ s
            pos = 0
            for a, source in enumerate((x, dy)):

                def visit(k, pos, a=a, source=source, s=s):
                    act(
                        pltpu.make_async_copy(
                            source.at[:, lanes(k, size)],
                            sends[s - 1].at[pos],
                            sem.at[s - 1, a * per_slice + k],
                        )
                    )

                pos = for_bits(meta[META_MASKS + 2 * target + a], me * per_slice, per_slice, pos, visit)

    visit_all(lambda copy: copy.start())
    visit_all(lambda copy: copy.wait())


def place_kernel(n, per_slice, meta, x, dy, *rest):
    recvs, targets, sem = rest[: n - 1], rest[n - 1 : n + 1], rest[n + 1]
    me = meta[META_ME]
    size = x.shape[-1] // per_slice

    def visit_all(act):
        for s in range(n):
            first = (me ^ s) * per_slice
            pos = 0
            for a, source in enumerate((x, dy)):

                def visit(k, pos, a=a, source=source, s=s, first=first):
                    block = source.at[:, lanes(k, size)] if s == 0 else recvs[s - 1].at[pos]
                    act(pltpu.make_async_copy(block, targets[a].at[first + k], sem.at[a, first + k]))

                pos = for_bits(meta[META_MASKS + 2 * me + a], first, per_slice, pos, visit)

    visit_all(lambda copy: copy.start())
    visit_all(lambda copy: copy.wait())


def load_needed(meta, sources, targets, sem, act):
    for a in (0, 1):

        def visit(k, pos, a=a):
            act(pltpu.make_async_copy(sources[a].at[k], targets[a].at[k], sem.at[a, k]))

        for_bits(meta[META_MASKS + 2 * meta[META_ME] + a], 0, targets[a].shape[0], 0, visit)


def entries_of(slots):
    return slots.shape[0] * slots.shape[2]


def slot_of(slots, e):
    return slots[lax.div(e, slots.shape[2]), 0, lax.rem(e, slots.shape[2])]


def entry_one(slots, e, feat_blocks, hid_blocks):
    s = slot_of(slots, e)
    return s < feat_blocks * hid_blocks, lax.div(s, hid_blocks), lax.rem(s, hid_blocks)


def entry_two(slots, e, feat_blocks, hid_blocks):
    s = slot_of(slots, e)
    return s < feat_blocks * hid_blocks, lax.rem(s, feat_blocks), lax.div(s, feat_blocks)


def active_hidden(slots_one, slots_two, feat_blocks, hid_blocks):
    def step(e, masks):
        found = []
        for mask, entry, slots in zip(masks, (entry_one, entry_two), (slots_one, slots_two)):
            live, _, h = entry(slots, e, feat_blocks, hid_blocks)
            found.append(mask | jnp.where(live, lax.shift_left(1, jnp.where(live, h, 0)), 0))
        return tuple(found)

    one, two = lax.fori_loop(0, entries_of(slots_one), step, (0, 0), unroll=UNROLL)
    return one & two


def need_kernel(feat_blocks, hid_blocks, slots_one, slots_two, out):
    active = active_hidden(slots_one, slots_two, feat_blocks, hid_blocks)

    def step(e, masks):
        found = []
        for mask, entry, slots in zip(masks, (entry_one, entry_two), (slots_one, slots_two)):
            live, f, h = entry(slots, e, feat_blocks, hid_blocks)
            wanted = live & (bit_of(active, jnp.where(live, h, 0)) == 1)
            found.append(mask | jnp.where(wanted, lax.shift_left(1, jnp.where(wanted, f, 0)), 0))
        return tuple(found)

    out[0], out[1] = lax.fori_loop(0, entries_of(slots_one), step, (0, 0), unroll=UNROLL)


def ones(mask):
    shift = lax.shift_right_logical
    pairs = mask - (shift(mask, 1) & 0x55555555)
    fours = (pairs & 0x33333333) + (shift(pairs, 2) & 0x33333333)
    eights = (fours + shift(fours, 4)) & 0x0F0F0F0F
    sixteens = eights + shift(eights, 8)
    return (sixteens + shift(sixteens, 16)) & 63


def plan_kernel(n, per_slice, fetch_rows, back_rows, where, *rest):
    masks, meta, levels = rest[:n], rest[n], rest[n + 1]
    me = where[0]
    for k in range(3):
        meta[k] = where[k]
    for s in range(n):
        place = META_MASKS + 2 * (me ^ s)
        meta[place] = masks[s][0]
        meta[place + 1] = masks[s][1]
    low = (1 << per_slice) - 1
    most_fetch, most_back = [], []
    for s in range(1, n):

        def widest(i, most, s=s):
            place = META_MASKS + 2 * (i ^ s)
            counts = [ones(lax.shift_right_logical(meta[place + a], i * per_slice) & low) for a in (0, 1)]
            return jnp.maximum(most[0], counts[0] + counts[1]), jnp.maximum(most[1], counts[0])

        fetch, back = lax.fori_loop(0, n, widest, (0, 0))
        most_fetch.append(fetch)
        most_back.append(back)
    for k, (rows, most) in enumerate(((fetch_rows, most_fetch), (back_rows, most_back))):
        level = len(rows) - 1
        for r in range(len(rows) - 2, -1, -1):
            fits = most[0] <= rows[r][0]
            for s in range(1, n - 1):
                fits = fits & (most[s] <= rows[r][s])
            level = jnp.where(fits, r, level)
        levels[k] = level


def list_kernel(feat_blocks, hid_blocks, slots_one, slots_two, one, two):
    active = active_hidden(slots_one, slots_two, feat_blocks, hid_blocks)
    for entry, slots, listed in ((entry_one, slots_one, one), (entry_two, slots_two, two)):

        def step(e, count, entry=entry, slots=slots, listed=listed):
            live, f, h = entry(slots, e, feat_blocks, hid_blocks)
            h = jnp.where(live, h, 0)
            for k, value in enumerate((e, jnp.where(live, f, 0), h)):
                listed[k, count] = value
            return count + jnp.where(live, bit_of(active, h), 0)

        count = lax.fori_loop(0, entries_of(slots), step, 0)
        for k in range(GROUP - 1):
            for row, value in enumerate((0, feat_blocks, hid_blocks)):
                listed[row, count + k] = value
        listed[3, 0] = count
        listed[3, 1] = active


def groups(count):
    return lax.div(count + (GROUP - 1), GROUP)


def shard_kernel(n, per_slice, hid_blocks, meta, one, two, x, dy, w_one, w_two, *rest):
    own_out, keep_out, send_out = rest[:3]
    backs = rest[3 : n + 2]
    xs, dys, gxs, acts, pres, ones_in, twos_in, sem, back_sem, w_sem = rest[n + 2 :]
    per_owner = keep_out.shape[2]
    core, chip = meta[META_CORE], meta[META_CHIP]
    feat_blocks = xs.shape[0]
    me = meta[META_ME]
    size = xs.shape[-1]
    load = functools.partial(load_needed, meta, (x, dy), (xs, dys), sem)
    load(lambda copy: copy.start())
    weights = [
        pltpu.make_async_copy(source, target, w_sem.at[k])
        for k, (source, target) in enumerate(((w_one, ones_in), (w_two, twos_in)))
    ]
    for copy in weights:
        copy.start()
    count_one, count_two, active = one[3, 0], two[3, 0], one[3, 1]
    mask_x = meta[META_MASKS + 2 * me]

    def clear_hidden(h, pos):
        acts[h] = jnp.zeros(acts.shape[1:], jnp.float32)
        pres[h] = jnp.zeros(pres.shape[1:], jnp.float32)

    for_bits(active, 0, hid_blocks, 0, clear_hidden)

    def clear_feature(k, pos):
        gxs[k] = jnp.zeros(gxs.shape[1:], jnp.float32)

    for_bits(mask_x, 0, feat_blocks, 0, clear_feature)
    rows = 64

    def clear_own(k, carry):
        own_out[pl.ds(pl.multiple_of(rows * k, rows), rows)] = jnp.zeros((rows, own_out.shape[1]), jnp.float32)
        return carry

    lax.fori_loop(0, own_out.shape[0] // rows, clear_own, 0)

    def clear_blocks(k, carry):
        w, chip_at = lax.div(k, keep_out.shape[1]), lax.rem(k, keep_out.shape[1])
        for out in (keep_out, send_out):
            out[w, chip_at] = jnp.zeros(out.shape[2:], jnp.float32)
        return carry

    lax.fori_loop(0, 2 * keep_out.shape[1], clear_blocks, 0)
    load(lambda copy: copy.wait())
    for copy in weights:
        copy.wait()

    def accumulate(listed, count, product, into, target):
        def step(g, carry):
            entries = [[listed[row, GROUP * g + k] for row in range(3)] for k in range(GROUP)]
            terms = [product(e, f, h) for e, f, h in entries]
            for entry, term in zip(entries, terms):
                into[entry[target]] += term
            return carry

        lax.fori_loop(0, groups(count), step, 0)

    last = feat_blocks - 1
    accumulate(one, count_one, lambda e, f, h: dot_nn(xs[jnp.minimum(f, last)], ones_in[e]), acts, 2)
    accumulate(two, count_two, lambda e, f, h: dot_nt(dys[jnp.minimum(f, last)], twos_in[e]), pres, 2)

    def gelu(h, pos):
        pre_act = acts[h]
        cdf = 0.5 * (1.0 + lax.erf(pre_act * (1.0 / math.sqrt(2.0))))
        pdf = jnp.exp(-0.5 * pre_act * pre_act) * (1.0 / math.sqrt(2.0 * math.pi))
        acts[h] = pre_act * cdf
        pres[h] = pres[h] * (cdf + pre_act * pdf)

    for_bits(active, 0, hid_blocks, 0, gelu)
    accumulate(one, count_one, lambda e, f, h: dot_nt(pres[jnp.minimum(h, hid_blocks - 1)], ones_in[e]), gxs, 1)

    def send_back(act):
        for s in range(1, n):
            first = (me ^ s) * per_slice

            def visit(k, pos, s=s, first=first):
                act(pltpu.make_async_copy(gxs.at[first + k], backs[s - 1].at[pos], back_sem.at[first + k]))

            for_bits(mask_x, first, per_slice, 0, visit)

    send_back(lambda copy: copy.start())

    def keep(k, pos):
        own_out[:, lanes(k, size)] = gxs[me * per_slice + k]

    for_bits(mask_x, me * per_slice, per_slice, 0, keep)

    def fill(w, listed, count, product):
        def step(g, carry):
            places = [jnp.minimum(GROUP * g + k, count - 1) for k in range(GROUP)]
            entries = [[listed[row, place] for row in range(3)] for place in places]
            terms = [product(f, h) for _, f, h in entries]
            for (e, _, _), term in zip(entries, terms):
                owner, c = lax.div(e, per_owner), lax.rem(e, per_owner)
                where = lax.div(owner, 2) ^ chip
                mine = lax.rem(owner, 2) == core

                @pl.when(mine)
                def _(where=where, c=c, term=term):
                    keep_out[w, where, c] = term

                @pl.when(jnp.logical_not(mine))
                def _(where=where, c=c, term=term):
                    send_out[w, where, c] = term

            return carry

        lax.fori_loop(0, groups(count), step, 0)

    fill(0, one, count_one, lambda f, h: dot_tn(xs[f], pres[h]))
    fill(1, two, count_two, lambda f, h: dot_tn(acts[h], dys[f]))
    send_back(lambda copy: copy.wait())


def add_kernel(n, per_slice, meta, own, *rest):
    recvs, out, landed, sem = rest[: n - 1], rest[n - 1], rest[n], rest[n + 1]
    me = meta[META_ME]
    size = landed.shape[-1]

    def visit_all(visit):
        for s in range(1, n):
            mask = meta[META_MASKS + 2 * (me ^ s)]
            for_bits(mask, me * per_slice, per_slice, 0, functools.partial(visit, s - 1))

    def copy(place, k, pos):
        return pltpu.make_async_copy(recvs[place].at[pos], landed.at[place, k], sem.at[place, k])

    visit_all(lambda place, k, pos: copy(place, k, pos).start())
    out[...] = own[...]

    def add(place, k, pos):
        copy(place, k, pos).wait()
        out[:, lanes(k, size)] += landed[place, k]

    visit_all(add)


def kernel_call(kernel, name, *, out_shape, in_specs, out_specs, scratch_shapes=(), flops=0, moved=0):
    return pl.pallas_call(
        kernel,
        out_shape=out_shape,
        in_specs=in_specs,
        out_specs=out_specs,
        scratch_shapes=scratch_shapes,
        compiler_params=pltpu.CompilerParams(vmem_limit_bytes=VMEM_LIMIT),
        cost_estimate=pl.CostEstimate(flops=flops, bytes_accessed=moved, transcendentals=0),
        name=name,
    )


def kept_in(space, *arrays):
    return [pltpu.with_memory_space_constraint(array, space) for array in arrays]


def floats(*dims):
    return jax.ShapeDtypeStruct(dims, jnp.float32)


def rounds(n):
    return [[(k, k ^ r) for k in range(n)] for r in range(1, n)]


def fetch_blocks(caps, n, size, meta, x, dy):
    tokens, width = x.shape
    per_slice = width // size
    sends = kernel_call(
        functools.partial(pack_kernel, n, per_slice),
        "pack_blocks",
        out_shape=[pltpu.VMEM((cap, tokens, size), jnp.float32) for cap in caps],
        in_specs=[SMEM, ANY, ANY],
        out_specs=[ANY] * (n - 1),
        scratch_shapes=[pltpu.SemaphoreType.DMA((n - 1, 2 * per_slice))],
        moved=2 * 2**20,
    )(meta, *kept_in(pltpu.HBM, x, dy))
    recvs = [lax.ppermute(s, "ch", move) for s, move in zip(sends, rounds(n))]
    return kernel_call(
        functools.partial(place_kernel, n, per_slice),
        "place_blocks",
        out_shape=[floats(n * per_slice, tokens, size)] * 2,
        in_specs=[SMEM, VMEM, VMEM] + [ANY] * (n - 1),
        out_specs=[ANY] * 2,
        scratch_shapes=[pltpu.SemaphoreType.DMA((2, n * per_slice))],
        moved=2 * 2**20,
    )(meta, x, dy, *kept_in(pltpu.VMEM, *recvs))


def sum_over_chips(w, mine, m):
    steps = m.bit_length() - 1
    order = range(steps) if w == 0 else range(steps - 1, -1, -1)
    whole = mine.reshape((2,) * steps + mine.shape[1:])
    for k in order:
        axis = steps - 1 - k
        keep = lax.index_in_dim(whole, 0, axis, keepdims=True)
        send = lax.index_in_dim(whole, 1, axis, keepdims=True)
        whole = keep + lax.ppermute(send, "tok", [(t, t ^ (2 << k)) for t in range(2 * m)])
    return whole.reshape(mine.shape[1:])


def send_results(caps, n, m, meta, own, keep, send, *backs):
    tokens, width = own.shape
    size = keep.shape[-1]
    per_slice = width // size
    came = [lax.ppermute(b[:cap], "ch", move) for b, cap, move in zip(backs, caps, rounds(n))]
    grad_x = kernel_call(
        functools.partial(add_kernel, n, per_slice),
        "add_back",
        out_shape=floats(tokens, per_slice * size),
        in_specs=[SMEM, VMEM] + [ANY] * (n - 1),
        out_specs=VMEM,
        scratch_shapes=[
            pltpu.VMEM((n - 1, per_slice, tokens, size), jnp.float32),
            pltpu.SemaphoreType.DMA((n - 1, per_slice)),
        ],
    )(meta, own, *came)
    pairs = keep + lax.ppermute(send, "tok", [(t, t ^ 1) for t in range(2 * m)])
    return grad_x, *[sum_over_chips(w, pairs[w], m) for w in (0, 1)]


def body(inputs, grad_out, blocks_one, slots_one, blocks_two, slots_two):
    owners = blocks_one.shape[0]
    entries = blocks_one.shape[2]
    size = blocks_one.shape[-1]
    n, m = lax.axis_size("ch"), lax.axis_size("tok") // 2
    tokens, width = inputs.shape
    per_slice = width // size
    feat_blocks = per_slice * n
    hid_blocks = H // n // size
    w_one = blocks_one.reshape(owners * entries, size, size)
    w_two = blocks_two.reshape(owners * entries, size, size)
    ints = lambda count: jax.ShapeDtypeStruct((count,), jnp.int32)
    mine = kernel_call(
        functools.partial(need_kernel, feat_blocks, hid_blocks),
        "needed_features",
        out_shape=ints(2),
        in_specs=[SMEM] * 2,
        out_specs=SMEM,
    )(slots_one, slots_two)
    rows = jax.ShapeDtypeStruct((4, owners * entries + GROUP), jnp.int32)
    one, two = kernel_call(
        functools.partial(list_kernel, feat_blocks, hid_blocks),
        "list_entries",
        out_shape=[rows] * 2,
        in_specs=[SMEM] * 2,
        out_specs=[SMEM] * 2,
    )(slots_one, slots_two)
    masks = [mine] + [lax.ppermute(mine, "ch", move) for move in rounds(n)]
    tok = lax.axis_index("tok")
    where = jnp.stack([lax.axis_index("ch"), tok % 2, tok // 2]).astype(jnp.int32)
    fetch_rows = room(FETCH_ROWS, n, 2 * per_slice)
    back_rows = room(BACK_ROWS, n, per_slice)
    meta, levels = kernel_call(
        functools.partial(plan_kernel, n, per_slice, fetch_rows, back_rows),
        "plan",
        out_shape=[ints(META_MASKS + 2 * n), ints(2)],
        in_specs=[SMEM] * (n + 1),
        out_specs=[SMEM] * 2,
    )(where, *masks)
    xs, dys = lax.switch(
        levels[0], [functools.partial(fetch_blocks, row, n, size) for row in fetch_rows], meta, inputs, grad_out
    )
    own, keep, send, *backs = kernel_call(
        functools.partial(shard_kernel, n, per_slice, hid_blocks),
        "shard_blocks",
        out_shape=[
            floats(tokens, width),
            *[floats(2, m, entries, size, size)] * 2,
            *[pltpu.VMEM((per_slice, tokens, size), jnp.float32)] * (n - 1),
        ],
        in_specs=[SMEM] * 3 + [ANY] * 4,
        out_specs=[VMEM] * 3 + [ANY] * (n - 1),
        scratch_shapes=[
            pltpu.VMEM((feat_blocks, tokens, size), jnp.float32),
            pltpu.VMEM((feat_blocks, tokens, size), jnp.float32),
            pltpu.VMEM((feat_blocks + 1, tokens, size), jnp.float32),
            pltpu.VMEM((hid_blocks + 1, tokens, size), jnp.float32),
            pltpu.VMEM((hid_blocks + 1, tokens, size), jnp.float32),
            pltpu.VMEM(w_one.shape, jnp.float32),
            pltpu.VMEM(w_two.shape, jnp.float32),
            pltpu.SemaphoreType.DMA((2, feat_blocks)),
            pltpu.SemaphoreType.DMA((feat_blocks,)),
            pltpu.SemaphoreType.DMA((2,)),
        ],
        flops=5 * 10**9,
        moved=16 * 2**20,
    )(meta, one, two, xs, dys, *kept_in(pltpu.HBM, w_one, w_two))
    grad_x, sum_one, sum_two = lax.switch(
        levels[1],
        [functools.partial(send_results, row, n, m) for row in back_rows],
        meta,
        own,
        keep,
        send,
        *backs,
    )
    factor = 1.0 / math.sqrt(inputs.shape[0] * lax.axis_size("tok"))
    grad_one = (sum_one * factor).reshape(1, 1, entries, size, size)
    grad_two = (sum_two * factor).reshape(1, 1, entries, size, size)
    return (grad_x, grad_one, grad_two)


def solution(mesh):
    in_specs = (
        P("tok", "ch"),
        P("tok", "ch"),
        P(None, "ch", None, None, None),
        P(None, "ch", None),
        P(None, "ch", None, None, None),
        P(None, "ch", None),
    )
    out_specs = (P("tok", "ch"), P("tok", "ch", None, None, None), P("tok", "ch", None, None, None))
    return jax.shard_map(body, mesh=mesh, in_specs=in_specs, out_specs=out_specs, check_vma=False)
```

```python
import functools
import math

import jax
import jax.numpy as jnp
from jax import lax
from jax.experimental import pallas as pl
from jax.experimental.pallas import tpu as pltpu
from jax.sharding import PartitionSpec as P

H = 8192

VMEM_LIMIT = 36 * 2**20
ANY = pl.BlockSpec(memory_space=pl.ANY)
SMEM = pl.BlockSpec(memory_space=pltpu.SMEM)
VMEM = pl.BlockSpec(memory_space=pltpu.VMEM)
NN = (((1,), (0,)), ((), ()))
NT = (((1,), (1,)), ((), ()))
TN = (((0,), (0,)), ((), ()))

FETCH_ROWS = (
    (10, 6, 6),
    (11, 7, 6),
    (11, 6, 7),
    (12, 7, 7),
    (12, 8, 6),
    (13, 7, 8),
    (13, 6, 9),
    (14, 9, 7),
    (14, 8, 8),
    (15, 7, 10),
    (15, 10, 7),
    (16, 9, 9),
    (16, 8, 12),
    (16, 12, 8),
    (16, 11, 11),
    (16, 16, 16),
)
BACK_ROWS = (
    (6, 3, 4),
    (6, 4, 3),
    (7, 4, 4),
    (8, 4, 5),
    (8, 5, 4),
    (8, 5, 6),
    (8, 6, 5),
    (8, 8, 8),
)


def room(rows, n, most):
    bands = [0 if r < n // 2 else 1 + r % 2 for r in range(1, n)]
    full = max(max(row) for row in rows)
    sized = []
    for row in rows:
        caps = tuple(-(-row[b] * most // full) for b in bands)
        if caps not in sized:
            sized.append(caps)
    return sized


def split(value):
    high = value.astype(jnp.bfloat16)
    return high, (value - high.astype(jnp.float32)).astype(jnp.bfloat16)


def halves(value):
    return jnp.concatenate(split(value), axis=1)


def dot_wide(left, right, dims):
    return lax.dot_general(left, right, dims, preferred_element_type=jnp.float32)


def dot_nn(left, right):
    high, low = split(right)
    both = jnp.concatenate(
        [
            jnp.concatenate([high, low], axis=1),
            jnp.concatenate([high, jnp.zeros_like(low)], axis=1),
        ],
        axis=0,
    )
    out = dot_wide(halves(left), both, NN)
    size = right.shape[1]
    return out[:, :size] + out[:, size:]


def dot_nt(left, right):
    high, low = split(right)
    both = jnp.concatenate(
        [
            jnp.concatenate([high, high], axis=1),
            jnp.concatenate([low, jnp.zeros_like(low)], axis=1),
        ],
        axis=0,
    )
    out = dot_wide(halves(left), both, NT)
    size = right.shape[0]
    return out[:, :size] + out[:, size:]


def dot_tn(left, right):
    out = dot_wide(halves(left), halves(right), TN)
    rows, columns = left.shape[1], right.shape[1]
    return out[:rows, :columns] + (out[:rows, columns:] + out[rows:, :columns])


def bit_of(mask, place):
    return lax.shift_right_arithmetic(mask, place) & 1


def for_bits(mask, first, count, start, visit):
    def step(k, pos):
        bit = bit_of(mask, first + k)

        @pl.when(bit == 1)
        def _():
            visit(k, pos)

        return pos + bit

    return lax.fori_loop(0, count, step, start)


def lanes(block, size):
    return pl.ds(pl.multiple_of(block * size, size), size)


GROUP, PAIR = 4, 2
UNROLL = 8
META_ME, META_CORE, META_CHIP, META_MASKS = 0, 1, 2, 3


def pack_kernel(n, per_slice, meta, x, dy, *rest):
    sends, sem = rest[:-1], rest[-1]
    me = meta[META_ME]
    size = sends[0].shape[-1]

    def visit_all(act):
        for s in range(1, n):
            target = me ^ s
            pos = 0
            for a, source in enumerate((x, dy)):

                def visit(k, pos, a=a, source=source, s=s):
                    act(
                        pltpu.make_async_copy(
                            source.at[:, lanes(k, size)],
                            sends[s - 1].at[pos],
                            sem.at[s - 1, a * per_slice + k],
                        )
                    )

                pos = for_bits(meta[META_MASKS + 2 * target + a], me * per_slice, per_slice, pos, visit)

    visit_all(lambda copy: copy.start())
    visit_all(lambda copy: copy.wait())


def place_kernel(n, per_slice, meta, x, dy, *rest):
    recvs, targets, sem = rest[: n - 1], rest[n - 1 : n + 1], rest[n + 1]
    me = meta[META_ME]
    size = x.shape[-1] // per_slice

    def visit_all(act):
        for s in range(n):
            first = (me ^ s) * per_slice
            pos = 0
            for a, source in enumerate((x, dy)):

                def visit(k, pos, a=a, source=source, s=s, first=first):
                    block = source.at[:, lanes(k, size)] if s == 0 else recvs[s - 1].at[pos]
                    act(pltpu.make_async_copy(block, targets[a].at[first + k], sem.at[a, first + k]))

                pos = for_bits(meta[META_MASKS + 2 * me + a], first, per_slice, pos, visit)

    visit_all(lambda copy: copy.start())
    visit_all(lambda copy: copy.wait())


def load_needed(meta, sources, targets, sem, act):
    for a in (0, 1):

        def visit(k, pos, a=a):
            act(pltpu.make_async_copy(sources[a].at[k], targets[a].at[k], sem.at[a, k]))

        for_bits(meta[META_MASKS + 2 * meta[META_ME] + a], 0, targets[a].shape[0], 0, visit)


def entries_of(slots):
    return slots.shape[0] * slots.shape[2]


def slot_of(slots, e):
    return slots[lax.div(e, slots.shape[2]), 0, lax.rem(e, slots.shape[2])]


def entry_one(slots, e, feat_blocks, hid_blocks):
    s = slot_of(slots, e)
    return s < feat_blocks * hid_blocks, lax.div(s, hid_blocks), lax.rem(s, hid_blocks)


def entry_two(slots, e, feat_blocks, hid_blocks):
    s = slot_of(slots, e)
    return s < feat_blocks * hid_blocks, lax.rem(s, feat_blocks), lax.div(s, feat_blocks)


def active_hidden(slots_one, slots_two, feat_blocks, hid_blocks):
    def step(e, masks):
        found = []
        for mask, entry, slots in zip(masks, (entry_one, entry_two), (slots_one, slots_two)):
            live, _, h = entry(slots, e, feat_blocks, hid_blocks)
            found.append(mask | jnp.where(live, lax.shift_left(1, jnp.where(live, h, 0)), 0))
        return tuple(found)

    one, two = lax.fori_loop(0, entries_of(slots_one), step, (0, 0), unroll=UNROLL)
    return one & two


def need_kernel(feat_blocks, hid_blocks, slots_one, slots_two, out):
    active = active_hidden(slots_one, slots_two, feat_blocks, hid_blocks)

    def step(e, masks):
        found = []
        for mask, entry, slots in zip(masks, (entry_one, entry_two), (slots_one, slots_two)):
            live, f, h = entry(slots, e, feat_blocks, hid_blocks)
            wanted = live & (bit_of(active, jnp.where(live, h, 0)) == 1)
            found.append(mask | jnp.where(wanted, lax.shift_left(1, jnp.where(wanted, f, 0)), 0))
        return tuple(found)

    out[0], out[1] = lax.fori_loop(0, entries_of(slots_one), step, (0, 0), unroll=UNROLL)


def ones(mask):
    shift = lax.shift_right_logical
    pairs = mask - (shift(mask, 1) & 0x55555555)
    fours = (pairs & 0x33333333) + (shift(pairs, 2) & 0x33333333)
    eights = (fours + shift(fours, 4)) & 0x0F0F0F0F
    sixteens = eights + shift(eights, 8)
    return (sixteens + shift(sixteens, 16)) & 63


def plan_kernel(n, per_slice, fetch_rows, back_rows, where, *rest):
    masks, meta, levels = rest[:n], rest[n], rest[n + 1]
    needed = functools.reduce(lax.bitwise_or, [mask[0] for mask in masks])
    levels[2] = jnp.where(needed != 0, 1, 0)
    me = where[0]
    for k in range(3):
        meta[k] = where[k]
    for s in range(n):
        place = META_MASKS + 2 * (me ^ s)
        meta[place] = masks[s][0]
        meta[place + 1] = masks[s][1]
    low = (1 << per_slice) - 1
    most_fetch, most_back = [], []
    for s in range(1, n):

        def widest(i, most, s=s):
            place = META_MASKS + 2 * (i ^ s)
            counts = [ones(lax.shift_right_logical(meta[place + a], i * per_slice) & low) for a in (0, 1)]
            return jnp.maximum(most[0], counts[0] + counts[1]), jnp.maximum(most[1], counts[0])

        fetch, back = lax.fori_loop(0, n, widest, (0, 0))
        most_fetch.append(fetch)
        most_back.append(back)
    for k, (rows, most) in enumerate(((fetch_rows, most_fetch), (back_rows, most_back))):
        level = len(rows) - 1
        for r in range(len(rows) - 2, -1, -1):
            fits = most[0] <= rows[r][0]
            for s in range(1, n - 1):
                fits = fits & (most[s] <= rows[r][s])
            level = jnp.where(fits, r, level)
        levels[k] = level


def list_kernel(feat_blocks, hid_blocks, slots_one, slots_two, one, two):
    active = active_hidden(slots_one, slots_two, feat_blocks, hid_blocks)
    for entry, slots, listed in ((entry_one, slots_one, one), (entry_two, slots_two, two)):

        def step(e, count, entry=entry, slots=slots, listed=listed):
            live, f, h = entry(slots, e, feat_blocks, hid_blocks)
            h = jnp.where(live, h, 0)
            for k, value in enumerate((e, jnp.where(live, f, 0), h)):
                listed[k, count] = value
            return count + jnp.where(live, bit_of(active, h), 0)

        count = lax.fori_loop(0, entries_of(slots), step, 0)
        for k in range(GROUP - 1):
            for row, value in enumerate((0, feat_blocks, hid_blocks)):
                listed[row, count + k] = value
        listed[3, 0] = count
        listed[3, 1] = active


def groups(count, group):
    return lax.div(count + (group - 1), group)


def shard_kernel(n, per_slice, hid_blocks, meta, one, two, x, dy, w_one, w_two, *rest):
    own_out, acts, pres = rest[:3]
    backs = rest[3 : n + 2]
    xs, dys, gxs, ones_in, twos_in, sem, back_sem, w_sem = rest[n + 2 :]
    feat_blocks = xs.shape[0]
    me = meta[META_ME]
    size = xs.shape[-1]
    load = functools.partial(load_needed, meta, (x, dy), (xs, dys), sem)
    load(lambda copy: copy.start())
    weights = [
        pltpu.make_async_copy(source, target, w_sem.at[k])
        for k, (source, target) in enumerate(((w_one, ones_in), (w_two, twos_in)))
    ]
    for copy in weights:
        copy.start()
    count_one, count_two, active = one[3, 0], two[3, 0], one[3, 1]
    mask_x = meta[META_MASKS + 2 * me]

    def clear_hidden(h, pos):
        acts[h] = jnp.zeros(acts.shape[1:], jnp.float32)
        pres[h] = jnp.zeros(pres.shape[1:], jnp.float32)

    for_bits(active, 0, hid_blocks, 0, clear_hidden)

    def clear_feature(k, pos):
        gxs[k] = jnp.zeros(gxs.shape[1:], jnp.float32)

    for_bits(mask_x, 0, feat_blocks, 0, clear_feature)
    rows = 64

    def clear_own(k, carry):
        own_out[pl.ds(pl.multiple_of(rows * k, rows), rows)] = jnp.zeros((rows, own_out.shape[1]), jnp.float32)
        return carry

    lax.fori_loop(0, own_out.shape[0] // rows, clear_own, 0)

    load(lambda copy: copy.wait())
    for copy in weights:
        copy.wait()

    def accumulate(listed, count, product, into, target):
        def step(g, carry):
            entries = [[listed[row, GROUP * g + k] for row in range(3)] for k in range(GROUP)]
            terms = [product(e, f, h) for e, f, h in entries]
            for entry, term in zip(entries, terms):
                into[entry[target]] += term
            return carry

        lax.fori_loop(0, groups(count, GROUP), step, 0)

    last = feat_blocks - 1
    accumulate(one, count_one, lambda e, f, h: dot_nn(xs[jnp.minimum(f, last)], ones_in[e]), acts, 2)
    accumulate(two, count_two, lambda e, f, h: dot_nt(dys[jnp.minimum(f, last)], twos_in[e]), pres, 2)

    def gelu(h, pos):
        pre_act = acts[h]
        cdf = 0.5 * (1.0 + lax.erf(pre_act * (1.0 / math.sqrt(2.0))))
        pdf = jnp.exp(-0.5 * pre_act * pre_act) * (1.0 / math.sqrt(2.0 * math.pi))
        acts[h] = pre_act * cdf
        pres[h] = pres[h] * (cdf + pre_act * pdf)

    for_bits(active, 0, hid_blocks, 0, gelu)
    accumulate(one, count_one, lambda e, f, h: dot_nt(pres[jnp.minimum(h, hid_blocks - 1)], ones_in[e]), gxs, 1)

    def send_back(act):
        for s in range(1, n):
            first = (me ^ s) * per_slice

            def visit(k, pos, s=s, first=first):
                act(pltpu.make_async_copy(gxs.at[first + k], backs[s - 1].at[pos], back_sem.at[first + k]))

            for_bits(mask_x, first, per_slice, 0, visit)

    send_back(lambda copy: copy.start())

    def keep(k, pos):
        own_out[:, lanes(k, size)] = gxs[me * per_slice + k]

    for_bits(mask_x, me * per_slice, per_slice, 0, keep)
    send_back(lambda copy: copy.wait())


def blocks_kernel(hid_blocks, meta, one, two, x, dy, acts, pres, keep_out, send_out, xs, dys, sem):
    per_owner = keep_out.shape[2]
    core, chip = meta[META_CORE], meta[META_CHIP]
    count_one, count_two = one[3, 0], two[3, 0]
    load = functools.partial(load_needed, meta, (x, dy), (xs, dys), sem)
    load(lambda copy: copy.start())

    def clear_blocks(k, carry):
        w, chip_at = lax.div(k, keep_out.shape[1]), lax.rem(k, keep_out.shape[1])
        for out in (keep_out, send_out):
            out[w, chip_at] = jnp.zeros(out.shape[2:], jnp.float32)
        return carry

    lax.fori_loop(0, 2 * keep_out.shape[1], clear_blocks, 0)
    load(lambda copy: copy.wait())

    def fill(w, listed, count, product):
        def step(g, carry):
            places = [jnp.minimum(PAIR * g + k, count - 1) for k in range(PAIR)]
            entries = [[listed[row, place] for row in range(3)] for place in places]
            terms = [product(f, h) for _, f, h in entries]
            for (e, _, _), term in zip(entries, terms):
                owner, c = lax.div(e, per_owner), lax.rem(e, per_owner)
                where = lax.div(owner, 2) ^ chip
                mine = lax.rem(owner, 2) == core

                @pl.when(mine)
                def _(where=where, c=c, term=term):
                    keep_out[w, where, c] = term

                @pl.when(jnp.logical_not(mine))
                def _(where=where, c=c, term=term):
                    send_out[w, where, c] = term

            return carry

        lax.fori_loop(0, groups(count, PAIR), step, 0)

    fill(0, one, count_one, lambda f, h: dot_tn(xs[f], pres[h]))
    fill(1, two, count_two, lambda f, h: dot_tn(acts[h], dys[f]))


def add_kernel(n, per_slice, meta, own, *rest):
    recvs, out, landed, sem = rest[: n - 1], rest[n - 1], rest[n], rest[n + 1]
    me = meta[META_ME]
    size = landed.shape[-1]

    def visit_all(visit):
        for s in range(1, n):
            mask = meta[META_MASKS + 2 * (me ^ s)]
            for_bits(mask, me * per_slice, per_slice, 0, functools.partial(visit, s - 1))

    def copy(place, k, pos):
        return pltpu.make_async_copy(recvs[place].at[pos], landed.at[place, k], sem.at[place, k])

    visit_all(lambda place, k, pos: copy(place, k, pos).start())
    out[...] = own[...]

    def add(place, k, pos):
        copy(place, k, pos).wait()
        out[:, lanes(k, size)] += landed[place, k]

    visit_all(add)


def kernel_call(kernel, name, *, out_shape, in_specs, out_specs, scratch_shapes=(), flops=0, moved=0):
    return pl.pallas_call(
        kernel,
        out_shape=out_shape,
        in_specs=in_specs,
        out_specs=out_specs,
        scratch_shapes=scratch_shapes,
        compiler_params=pltpu.CompilerParams(vmem_limit_bytes=VMEM_LIMIT),
        cost_estimate=pl.CostEstimate(flops=flops, bytes_accessed=moved, transcendentals=0),
        name=name,
    )


def kept_in(space, *arrays):
    return [pltpu.with_memory_space_constraint(array, space) for array in arrays]


def floats(*dims):
    return jax.ShapeDtypeStruct(dims, jnp.float32)


def rounds(n):
    return [[(k, k ^ r) for k in range(n)] for r in range(1, n)]


def fetch_blocks(caps, n, size, meta, x, dy):
    tokens, width = x.shape
    per_slice = width // size
    sends = kernel_call(
        functools.partial(pack_kernel, n, per_slice),
        "pack_blocks",
        out_shape=[pltpu.VMEM((cap, tokens, size), jnp.float32) for cap in caps],
        in_specs=[SMEM, ANY, ANY],
        out_specs=[ANY] * (n - 1),
        scratch_shapes=[pltpu.SemaphoreType.DMA((n - 1, 2 * per_slice))],
        moved=2 * 2**20,
    )(meta, *kept_in(pltpu.HBM, x, dy))
    recvs = [lax.ppermute(s, "ch", move) for s, move in zip(sends, rounds(n))]
    return kernel_call(
        functools.partial(place_kernel, n, per_slice),
        "place_blocks",
        out_shape=[floats(n * per_slice, tokens, size)] * 2,
        in_specs=[SMEM, VMEM, VMEM] + [ANY] * (n - 1),
        out_specs=[ANY] * 2,
        scratch_shapes=[pltpu.SemaphoreType.DMA((2, n * per_slice))],
        moved=2 * 2**20,
    )(meta, x, dy, *kept_in(pltpu.VMEM, *recvs))


def sum_over_chips(w, mine, m):
    steps = m.bit_length() - 1
    order = range(steps) if w == 0 else range(steps - 1, -1, -1)
    whole = mine.reshape((2,) * steps + mine.shape[1:])
    for k in order:
        axis = steps - 1 - k
        keep = lax.index_in_dim(whole, 0, axis, keepdims=True)
        send = lax.index_in_dim(whole, 1, axis, keepdims=True)
        whole = keep + lax.ppermute(send, "tok", [(t, t ^ (2 << k)) for t in range(2 * m)])
    return whole.reshape(mine.shape[1:])


def send_results(caps, n, m, hid_blocks, per_owner, factor, any_needed, meta, one, two, xs, dys, acts, pres, own, *backs):
    tokens, width = own.shape
    size = xs.shape[-1]
    per_slice = width // size
    came = [lax.ppermute(b[:cap], "ch", move) for b, cap, move in zip(backs, caps, rounds(n))]
    grad_x = kernel_call(
        functools.partial(add_kernel, n, per_slice),
        "add_back",
        out_shape=floats(tokens, per_slice * size),
        in_specs=[SMEM, VMEM] + [ANY] * (n - 1),
        out_specs=VMEM,
        scratch_shapes=[
            pltpu.VMEM((n - 1, per_slice, tokens, size), jnp.float32),
            pltpu.SemaphoreType.DMA((n - 1, per_slice)),
        ],
    )(meta, own, *came)
    sums = lax.cond(
        any_needed > 0,
        functools.partial(gradient_blocks, m, hid_blocks, per_owner, factor),
        lambda *operands: [jnp.zeros((per_owner, size, size), own.dtype)] * 2,
        meta,
        one,
        two,
        xs,
        dys,
        acts,
        pres,
    )
    return grad_x, *sums


def gradient_blocks(m, hid_blocks, per_owner, factor, meta, one, two, xs, dys, acts, pres):
    feat_blocks, _, size = xs.shape
    keep, send = kernel_call(
        functools.partial(blocks_kernel, hid_blocks),
        "gradient_blocks",
        out_shape=[floats(2, m, per_owner, size, size)] * 2,
        in_specs=[SMEM] * 3 + [ANY] * 2 + [VMEM] * 2,
        out_specs=[VMEM] * 2,
        scratch_shapes=[
            pltpu.VMEM(xs.shape, jnp.float32),
            pltpu.VMEM(xs.shape, jnp.float32),
            pltpu.SemaphoreType.DMA((2, feat_blocks)),
        ],
        flops=2 * 10**9,
        moved=16 * 2**20,
    )(meta, one, two, xs, dys, acts, pres)
    return sum_over_tokens(m, factor, keep, send)


def sum_over_tokens(m, factor, keep, send):
    pairs = keep + lax.ppermute(send, "tok", [(t, t ^ 1) for t in range(2 * m)])
    return [sum_over_chips(w, pairs[w], m) * factor for w in (0, 1)]


def body(inputs, grad_out, blocks_one, slots_one, blocks_two, slots_two):
    owners = blocks_one.shape[0]
    entries = blocks_one.shape[2]
    size = blocks_one.shape[-1]
    n, m = lax.axis_size("ch"), lax.axis_size("tok") // 2
    tokens, width = inputs.shape
    per_slice = width // size
    feat_blocks = per_slice * n
    hid_blocks = H // n // size
    w_one = blocks_one.reshape(owners * entries, size, size)
    w_two = blocks_two.reshape(owners * entries, size, size)
    ints = lambda count: jax.ShapeDtypeStruct((count,), jnp.int32)
    mine = kernel_call(
        functools.partial(need_kernel, feat_blocks, hid_blocks),
        "needed_features",
        out_shape=ints(2),
        in_specs=[SMEM] * 2,
        out_specs=SMEM,
    )(slots_one, slots_two)
    rows = jax.ShapeDtypeStruct((4, owners * entries + GROUP), jnp.int32)
    one, two = kernel_call(
        functools.partial(list_kernel, feat_blocks, hid_blocks),
        "list_entries",
        out_shape=[rows] * 2,
        in_specs=[SMEM] * 2,
        out_specs=[SMEM] * 2,
    )(slots_one, slots_two)
    masks = [mine] + [lax.ppermute(mine, "ch", move) for move in rounds(n)]
    tok = lax.axis_index("tok")
    where = jnp.stack([lax.axis_index("ch"), tok % 2, tok // 2]).astype(jnp.int32)
    fetch_rows = room(FETCH_ROWS, n, 2 * per_slice)
    back_rows = room(BACK_ROWS, n, per_slice)
    meta, levels = kernel_call(
        functools.partial(plan_kernel, n, per_slice, fetch_rows, back_rows),
        "plan",
        out_shape=[ints(META_MASKS + 2 * n), ints(3)],
        in_specs=[SMEM] * (n + 1),
        out_specs=[SMEM] * 2,
    )(where, *masks)
    xs, dys = lax.switch(
        levels[0], [functools.partial(fetch_blocks, row, n, size) for row in fetch_rows], meta, inputs, grad_out
    )
    own, acts, pres, *backs = kernel_call(
        functools.partial(shard_kernel, n, per_slice, hid_blocks),
        "shard_blocks",
        out_shape=[
            floats(tokens, width),
            *[floats(hid_blocks + 1, tokens, size)] * 2,
            *[pltpu.VMEM((per_slice, tokens, size), jnp.float32)] * (n - 1),
        ],
        in_specs=[SMEM] * 3 + [ANY] * 4,
        out_specs=[VMEM] * 3 + [ANY] * (n - 1),
        scratch_shapes=[
            pltpu.VMEM((feat_blocks, tokens, size), jnp.float32),
            pltpu.VMEM((feat_blocks, tokens, size), jnp.float32),
            pltpu.VMEM((feat_blocks + 1, tokens, size), jnp.float32),
            pltpu.VMEM(w_one.shape, jnp.float32),
            pltpu.VMEM(w_two.shape, jnp.float32),
            pltpu.SemaphoreType.DMA((2, feat_blocks)),
            pltpu.SemaphoreType.DMA((feat_blocks,)),
            pltpu.SemaphoreType.DMA((2,)),
        ],
        flops=5 * 10**9,
        moved=16 * 2**20,
    )(meta, one, two, xs, dys, *kept_in(pltpu.HBM, w_one, w_two))
    factor = 1.0 / math.sqrt(inputs.shape[0] * lax.axis_size("tok"))
    grad_x, grad_one, grad_two = lax.switch(
        levels[1],
        [functools.partial(send_results, row, n, m, hid_blocks, entries, factor) for row in back_rows],
        levels[2],
        meta,
        one,
        two,
        xs,
        dys,
        acts,
        pres,
        own,
        *backs,
    )
    grad_one = grad_one.reshape(1, 1, entries, size, size)
    grad_two = grad_two.reshape(1, 1, entries, size, size)
    return (grad_x, grad_one, grad_two)


def solution(mesh):
    in_specs = (
        P("tok", "ch"),
        P("tok", "ch"),
        P(None, "ch", None, None, None),
        P(None, "ch", None),
        P(None, "ch", None, None, None),
        P(None, "ch", None),
    )
    out_specs = (P("tok", "ch"), P("tok", "ch", None, None, None), P("tok", "ch", None, None, None))
    return jax.shard_map(body, mesh=mesh, in_specs=in_specs, out_specs=out_specs, check_vma=False)
```

```python
import functools
import math

import jax
import jax.numpy as jnp
from jax import lax
from jax.experimental import pallas as pl
from jax.experimental.pallas import tpu as pltpu
from jax.sharding import PartitionSpec as P

H = 8192

VMEM_LIMIT = 36 * 2**20
ANY = pl.BlockSpec(memory_space=pl.ANY)
SMEM = pl.BlockSpec(memory_space=pltpu.SMEM)
VMEM = pl.BlockSpec(memory_space=pltpu.VMEM)
NN = (((1,), (0,)), ((), ()))
NT = (((1,), (1,)), ((), ()))
TN = (((0,), (0,)), ((), ()))

FETCH_ROWS = (
    (10, 6, 6),
    (11, 7, 6),
    (11, 6, 7),
    (12, 7, 7),
    (12, 8, 6),
    (13, 7, 8),
    (13, 6, 9),
    (14, 9, 7),
    (14, 8, 8),
    (15, 7, 10),
    (15, 10, 7),
    (16, 9, 9),
    (16, 8, 12),
    (16, 12, 8),
    (16, 11, 11),
    (16, 16, 16),
)
BACK_ROWS = (
    (6, 3, 4),
    (6, 4, 3),
    (7, 4, 4),
    (8, 4, 5),
    (8, 5, 4),
    (8, 5, 6),
    (8, 6, 5),
    (8, 8, 8),
)


def room(rows, n, most):
    bands = [0 if r < n // 2 else 1 + r % 2 for r in range(1, n)]
    full = max(max(row) for row in rows)
    sized = []
    for row in rows:
        caps = tuple(-(-row[b] * most // full) for b in bands)
        if caps not in sized:
            sized.append(caps)
    return sized


def split(value):
    high = value.astype(jnp.bfloat16)
    return high, (value - high.astype(jnp.float32)).astype(jnp.bfloat16)


def halves(value):
    return jnp.concatenate(split(value), axis=1)


def dot_wide(left, right, dims):
    return lax.dot_general(left, right, dims, preferred_element_type=jnp.float32)


def dot_nn(left, right):
    high, low = split(right)
    both = jnp.concatenate(
        [
            jnp.concatenate([high, low], axis=1),
            jnp.concatenate([high, jnp.zeros_like(low)], axis=1),
        ],
        axis=0,
    )
    out = dot_wide(halves(left), both, NN)
    size = right.shape[1]
    return out[:, :size] + out[:, size:]


def dot_nt(left, right):
    high, low = split(right)
    both = jnp.concatenate(
        [
            jnp.concatenate([high, high], axis=1),
            jnp.concatenate([low, jnp.zeros_like(low)], axis=1),
        ],
        axis=0,
    )
    out = dot_wide(halves(left), both, NT)
    size = right.shape[0]
    return out[:, :size] + out[:, size:]


def dot_tn(left, right):
    out = dot_wide(halves(left), halves(right), TN)
    rows, columns = left.shape[1], right.shape[1]
    return out[:rows, :columns] + (out[:rows, columns:] + out[rows:, :columns])


def bit_of(mask, place):
    return lax.shift_right_arithmetic(mask, place) & 1


def for_bits(mask, first, count, start, visit):
    def step(k, pos):
        bit = bit_of(mask, first + k)

        @pl.when(bit == 1)
        def _():
            visit(k, pos)

        return pos + bit

    return lax.fori_loop(0, count, step, start)


def lanes(block, size):
    return pl.ds(pl.multiple_of(block * size, size), size)


GROUP, PAIR = 4, 2
UNROLL = 8
META_ME, META_CORE, META_CHIP, META_MASKS = 0, 1, 2, 3


def pack_kernel(n, per_slice, meta, x, dy, *rest):
    sends, sem = rest[:-1], rest[-1]
    me = meta[META_ME]
    size = sends[0].shape[-1]

    def visit_all(act):
        for s in range(1, n):
            target = me ^ s
            pos = 0
            for a, source in enumerate((x, dy)):

                def visit(k, pos, a=a, source=source, s=s):
                    act(
                        pltpu.make_async_copy(
                            source.at[:, lanes(k, size)],
                            sends[s - 1].at[pos],
                            sem.at[s - 1, a * per_slice + k],
                        )
                    )

                pos = for_bits(meta[META_MASKS + 2 * target + a], me * per_slice, per_slice, pos, visit)

    visit_all(lambda copy: copy.start())
    visit_all(lambda copy: copy.wait())


def place_kernel(n, per_slice, meta, x, dy, *rest):
    recvs, targets, sem = rest[: n - 1], rest[n - 1 : n + 1], rest[n + 1]
    me = meta[META_ME]
    size = x.shape[-1] // per_slice

    def visit_all(act):
        for s in range(n):
            first = (me ^ s) * per_slice
            pos = 0
            for a, source in enumerate((x, dy)):

                def visit(k, pos, a=a, source=source, s=s, first=first):
                    block = source.at[:, lanes(k, size)] if s == 0 else recvs[s - 1].at[pos]
                    act(pltpu.make_async_copy(block, targets[a].at[first + k], sem.at[a, first + k]))

                pos = for_bits(meta[META_MASKS + 2 * me + a], first, per_slice, pos, visit)

    visit_all(lambda copy: copy.start())
    visit_all(lambda copy: copy.wait())


def load_needed(meta, sources, targets, sem, act):
    for a in (0, 1):

        def visit(k, pos, a=a):
            act(pltpu.make_async_copy(sources[a].at[k], targets[a].at[k], sem.at[a, k]))

        for_bits(meta[META_MASKS + 2 * meta[META_ME] + a], 0, targets[a].shape[0], 0, visit)


def quotient(value, by):
    if by & (by - 1) == 0:
        return lax.shift_right_logical(value, by.bit_length() - 1), value & (by - 1)
    return lax.div(value, by), lax.rem(value, by)


def entries_of(slots):
    return slots.shape[0] * slots.shape[2]


def slot_of(slots, w, e):
    owner, c = quotient(e, slots.shape[2])
    return slots[owner, w, c]


def entry_one(slots, e, feat_blocks, hid_blocks):
    s = slot_of(slots, 0, e)
    f, h = quotient(s, hid_blocks)
    return s < feat_blocks * hid_blocks, f, h


def entry_two(slots, e, feat_blocks, hid_blocks):
    s = slot_of(slots, 1, e)
    h, f = quotient(s, feat_blocks)
    return s < feat_blocks * hid_blocks, f, h


def active_hidden(slots, feat_blocks, hid_blocks):
    def step(e, masks):
        found = []
        for mask, entry in zip(masks, (entry_one, entry_two)):
            live, _, h = entry(slots, e, feat_blocks, hid_blocks)
            found.append(mask | jnp.where(live, lax.shift_left(1, jnp.where(live, h, 0)), 0))
        return tuple(found)

    one, two = lax.fori_loop(0, entries_of(slots), step, (0, 0), unroll=UNROLL)
    return one & two


def need_kernel(feat_blocks, hid_blocks, slots, out):
    active = active_hidden(slots, feat_blocks, hid_blocks)

    def step(e, masks):
        found = []
        for mask, entry in zip(masks, (entry_one, entry_two)):
            live, f, h = entry(slots, e, feat_blocks, hid_blocks)
            wanted = live & (bit_of(active, jnp.where(live, h, 0)) == 1)
            found.append(mask | jnp.where(wanted, lax.shift_left(1, jnp.where(wanted, f, 0)), 0))
        return tuple(found)

    out[0], out[1] = lax.fori_loop(0, entries_of(slots), step, (0, 0), unroll=UNROLL)


def ones(mask):
    shift = lax.shift_right_logical
    pairs = mask - (shift(mask, 1) & 0x55555555)
    fours = (pairs & 0x33333333) + (shift(pairs, 2) & 0x33333333)
    eights = (fours + shift(fours, 4)) & 0x0F0F0F0F
    sixteens = eights + shift(eights, 8)
    return (sixteens + shift(sixteens, 16)) & 63


def plan_kernel(n, per_slice, fetch_rows, back_rows, where, *rest):
    masks, meta, levels = rest[:n], rest[n], rest[n + 1]
    needed = functools.reduce(lax.bitwise_or, [mask[0] for mask in masks])
    levels[2] = jnp.where(needed != 0, 1, 0)
    me = where[0]
    for k in range(3):
        meta[k] = where[k]
    for s in range(n):
        place = META_MASKS + 2 * (me ^ s)
        meta[place] = masks[s][0]
        meta[place + 1] = masks[s][1]
    low = (1 << per_slice) - 1
    most_fetch, most_back = [], []
    for s in range(1, n):

        def widest(i, most, s=s):
            place = META_MASKS + 2 * (i ^ s)
            counts = [ones(lax.shift_right_logical(meta[place + a], i * per_slice) & low) for a in (0, 1)]
            return jnp.maximum(most[0], counts[0] + counts[1]), jnp.maximum(most[1], counts[0])

        fetch, back = lax.fori_loop(0, n, widest, (0, 0))
        most_fetch.append(fetch)
        most_back.append(back)
    for k, (rows, most) in enumerate(((fetch_rows, most_fetch), (back_rows, most_back))):
        level = len(rows) - 1
        for r in range(len(rows) - 2, -1, -1):
            fits = most[0] <= rows[r][0]
            for s in range(1, n - 1):
                fits = fits & (most[s] <= rows[r][s])
            level = jnp.where(fits, r, level)
        levels[k] = level


def list_kernel(feat_blocks, hid_blocks, slots, one, two):
    active = active_hidden(slots, feat_blocks, hid_blocks)
    for entry, listed in ((entry_one, one), (entry_two, two)):

        def step(e, count, entry=entry, listed=listed):
            live, f, h = entry(slots, e, feat_blocks, hid_blocks)
            h = jnp.where(live, h, 0)
            for k, value in enumerate((e, jnp.where(live, f, 0), h)):
                listed[k, count] = value
            return count + jnp.where(live, bit_of(active, h), 0)

        count = lax.fori_loop(0, entries_of(slots), step, 0)
        for k in range(GROUP - 1):
            for row, value in enumerate((0, feat_blocks, hid_blocks)):
                listed[row, count + k] = value
        listed[3, 0] = count
        listed[3, 1] = active


def groups(count, group):
    return lax.div(count + (group - 1), group)


def shard_kernel(n, per_slice, hid_blocks, meta, one, two, x, dy, w_one, w_two, *rest):
    own_out, acts_out, pres_out = rest[:3]
    backs = rest[3 : n + 2]
    xs, dys, gxs, acts, pres, ones_in, twos_in, sem, back_sem, w_sem, hidden_sem = rest[n + 2 :]
    feat_blocks = xs.shape[0]
    me = meta[META_ME]
    size = xs.shape[-1]
    load = functools.partial(load_needed, meta, (x, dy), (xs, dys), sem)
    load(lambda copy: copy.start())
    weights = [
        pltpu.make_async_copy(source, target, w_sem.at[k])
        for k, (source, target) in enumerate(((w_one, ones_in), (w_two, twos_in)))
    ]
    for copy in weights:
        copy.start()
    count_one, count_two, active = one[3, 0], two[3, 0], one[3, 1]
    mask_x = meta[META_MASKS + 2 * me]

    def clear_hidden(h, pos):
        acts[h] = jnp.zeros(acts.shape[1:], jnp.float32)
        pres[h] = jnp.zeros(pres.shape[1:], jnp.float32)

    for_bits(active, 0, hid_blocks, 0, clear_hidden)

    def clear_feature(k, pos):
        gxs[k] = jnp.zeros(gxs.shape[1:], jnp.float32)

    for_bits(mask_x, 0, feat_blocks, 0, clear_feature)
    rows = 64

    def clear_own(k, carry):
        own_out[pl.ds(pl.multiple_of(rows * k, rows), rows)] = jnp.zeros((rows, own_out.shape[1]), jnp.float32)
        return carry

    lax.fori_loop(0, own_out.shape[0] // rows, clear_own, 0)

    load(lambda copy: copy.wait())
    for copy in weights:
        copy.wait()

    def accumulate(listed, count, product, into, target):
        def step(g, carry):
            entries = [[listed[row, GROUP * g + k] for row in range(3)] for k in range(GROUP)]
            terms = [product(e, f, h) for e, f, h in entries]
            for entry, term in zip(entries, terms):
                into[entry[target]] += term
            return carry

        lax.fori_loop(0, groups(count, GROUP), step, 0)

    last = feat_blocks - 1
    accumulate(one, count_one, lambda e, f, h: dot_nn(xs[jnp.minimum(f, last)], ones_in[e]), acts, 2)
    accumulate(two, count_two, lambda e, f, h: dot_nt(dys[jnp.minimum(f, last)], twos_in[e]), pres, 2)

    def gelu(h, pos):
        pre_act = acts[h]
        cdf = 0.5 * (1.0 + lax.erf(pre_act * (1.0 / math.sqrt(2.0))))
        pdf = jnp.exp(-0.5 * pre_act * pre_act) * (1.0 / math.sqrt(2.0 * math.pi))
        acts[h] = pre_act * cdf
        pres[h] = pres[h] * (cdf + pre_act * pdf)

    for_bits(active, 0, hid_blocks, 0, gelu)

    def hand_on(act):
        def visit(h, pos):
            for k, (source, target) in enumerate(((acts, acts_out), (pres, pres_out))):
                act(pltpu.make_async_copy(source.at[h], target.at[h], hidden_sem.at[k, h]))

        for_bits(active, 0, hid_blocks, 0, visit)

    hand_on(lambda copy: copy.start())
    accumulate(one, count_one, lambda e, f, h: dot_nt(pres[jnp.minimum(h, hid_blocks - 1)], ones_in[e]), gxs, 1)

    def send_back(act):
        for s in range(1, n):
            first = (me ^ s) * per_slice

            def visit(k, pos, s=s, first=first):
                act(pltpu.make_async_copy(gxs.at[first + k], backs[s - 1].at[pos], back_sem.at[first + k]))

            for_bits(mask_x, first, per_slice, 0, visit)

    send_back(lambda copy: copy.start())

    def keep(k, pos):
        own_out[:, lanes(k, size)] = gxs[me * per_slice + k]

    for_bits(mask_x, me * per_slice, per_slice, 0, keep)
    send_back(lambda copy: copy.wait())
    hand_on(lambda copy: copy.wait())


def blocks_kernel(hid_blocks, meta, one, two, x, dy, acts, pres, keep_out, send_out, xs, dys, sem):
    per_owner = keep_out.shape[2]
    core, chip = meta[META_CORE], meta[META_CHIP]
    count_one, count_two = one[3, 0], two[3, 0]
    load = functools.partial(load_needed, meta, (x, dy), (xs, dys), sem)
    load(lambda copy: copy.start())

    def clear_blocks(k, carry):
        w, chip_at = lax.div(k, keep_out.shape[1]), lax.rem(k, keep_out.shape[1])
        for out in (keep_out, send_out):
            out[w, chip_at] = jnp.zeros(out.shape[2:], jnp.float32)
        return carry

    lax.fori_loop(0, 2 * keep_out.shape[1], clear_blocks, 0)
    load(lambda copy: copy.wait())

    def fill(w, listed, count, product):
        def step(g, carry):
            places = [jnp.minimum(PAIR * g + k, count - 1) for k in range(PAIR)]
            entries = [[listed[row, place] for row in range(3)] for place in places]
            terms = [product(f, h) for _, f, h in entries]
            for (e, _, _), term in zip(entries, terms):
                owner, c = lax.div(e, per_owner), lax.rem(e, per_owner)
                where = lax.div(owner, 2) ^ chip
                mine = lax.rem(owner, 2) == core

                @pl.when(mine)
                def _(where=where, c=c, term=term):
                    keep_out[w, where, c] = term

                @pl.when(jnp.logical_not(mine))
                def _(where=where, c=c, term=term):
                    send_out[w, where, c] = term

            return carry

        lax.fori_loop(0, groups(count, PAIR), step, 0)

    fill(0, one, count_one, lambda f, h: dot_tn(xs[f], pres[h]))
    fill(1, two, count_two, lambda f, h: dot_tn(acts[h], dys[f]))


def add_kernel(n, per_slice, meta, own, *rest):
    recvs, out, landed, sem = rest[: n - 1], rest[n - 1], rest[n], rest[n + 1]
    me = meta[META_ME]
    size = landed.shape[-1]

    def visit_all(visit):
        for s in range(1, n):
            mask = meta[META_MASKS + 2 * (me ^ s)]
            for_bits(mask, me * per_slice, per_slice, 0, functools.partial(visit, s - 1))

    def copy(place, k, pos):
        return pltpu.make_async_copy(recvs[place].at[pos], landed.at[place, k], sem.at[place, k])

    visit_all(lambda place, k, pos: copy(place, k, pos).start())
    out[...] = own[...]

    def add(place, k, pos):
        copy(place, k, pos).wait()
        out[:, lanes(k, size)] += landed[place, k]

    visit_all(add)


def kernel_call(kernel, name, *, out_shape, in_specs, out_specs, scratch_shapes=(), flops=0, moved=0):
    return pl.pallas_call(
        kernel,
        out_shape=out_shape,
        in_specs=in_specs,
        out_specs=out_specs,
        scratch_shapes=scratch_shapes,
        compiler_params=pltpu.CompilerParams(vmem_limit_bytes=VMEM_LIMIT),
        cost_estimate=pl.CostEstimate(flops=flops, bytes_accessed=moved, transcendentals=0),
        name=name,
    )


def kept_in(space, *arrays):
    return [pltpu.with_memory_space_constraint(array, space) for array in arrays]


def floats(*dims):
    return jax.ShapeDtypeStruct(dims, jnp.float32)


def rounds(n):
    return [[(k, k ^ r) for k in range(n)] for r in range(1, n)]


def fetch_blocks(caps, n, size, meta, x, dy):
    tokens, width = x.shape
    per_slice = width // size
    sends = kernel_call(
        functools.partial(pack_kernel, n, per_slice),
        "pack_blocks",
        out_shape=[pltpu.VMEM((cap, tokens, size), jnp.float32) for cap in caps],
        in_specs=[SMEM, ANY, ANY],
        out_specs=[ANY] * (n - 1),
        scratch_shapes=[pltpu.SemaphoreType.DMA((n - 1, 2 * per_slice))],
        moved=2 * 2**20,
    )(meta, *kept_in(pltpu.HBM, x, dy))
    recvs = [lax.ppermute(s, "ch", move) for s, move in zip(sends, rounds(n))]
    return kernel_call(
        functools.partial(place_kernel, n, per_slice),
        "place_blocks",
        out_shape=[floats(n * per_slice, tokens, size)] * 2,
        in_specs=[SMEM, VMEM, VMEM] + [ANY] * (n - 1),
        out_specs=[ANY] * 2,
        scratch_shapes=[pltpu.SemaphoreType.DMA((2, n * per_slice))],
        moved=2 * 2**20,
    )(meta, x, dy, *kept_in(pltpu.VMEM, *recvs))


def sum_over_chips(w, mine, m):
    steps = m.bit_length() - 1
    order = range(steps) if w == 0 else range(steps - 1, -1, -1)
    whole = mine.reshape((2,) * steps + mine.shape[1:])
    for k in order:
        axis = steps - 1 - k
        keep = lax.index_in_dim(whole, 0, axis, keepdims=True)
        send = lax.index_in_dim(whole, 1, axis, keepdims=True)
        whole = keep + lax.ppermute(send, "tok", [(t, t ^ (2 << k)) for t in range(2 * m)])
    return whole.reshape(mine.shape[1:])


def send_results(caps, n, m, hid_blocks, per_owner, factor, any_needed, meta, one, two, xs, dys, acts, pres, own, *backs):
    tokens, width = own.shape
    size = xs.shape[-1]
    per_slice = width // size
    came = [lax.ppermute(b[:cap], "ch", move) for b, cap, move in zip(backs, caps, rounds(n))]
    grad_x = kernel_call(
        functools.partial(add_kernel, n, per_slice),
        "add_back",
        out_shape=floats(tokens, per_slice * size),
        in_specs=[SMEM, VMEM] + [ANY] * (n - 1),
        out_specs=VMEM,
        scratch_shapes=[
            pltpu.VMEM((n - 1, per_slice, tokens, size), jnp.float32),
            pltpu.SemaphoreType.DMA((n - 1, per_slice)),
        ],
    )(meta, own, *came)
    sums = lax.cond(
        any_needed > 0,
        functools.partial(gradient_blocks, m, hid_blocks, per_owner, factor),
        lambda *operands: [jnp.zeros((per_owner, size, size), own.dtype)] * 2,
        meta,
        one,
        two,
        xs,
        dys,
        acts,
        pres,
    )
    return grad_x, *sums


def gradient_blocks(m, hid_blocks, per_owner, factor, meta, one, two, xs, dys, acts, pres):
    feat_blocks, _, size = xs.shape
    keep, send = kernel_call(
        functools.partial(blocks_kernel, hid_blocks),
        "gradient_blocks",
        out_shape=[floats(2, m, per_owner, size, size)] * 2,
        in_specs=[SMEM] * 3 + [ANY] * 2 + [VMEM] * 2,
        out_specs=[VMEM] * 2,
        scratch_shapes=[
            pltpu.VMEM(xs.shape, jnp.float32),
            pltpu.VMEM(xs.shape, jnp.float32),
            pltpu.SemaphoreType.DMA((2, feat_blocks)),
        ],
        flops=2 * 10**9,
        moved=16 * 2**20,
    )(meta, one, two, xs, dys, acts, pres)
    return sum_over_tokens(m, factor, keep, send)


def sum_over_tokens(m, factor, keep, send):
    pairs = keep + lax.ppermute(send, "tok", [(t, t ^ 1) for t in range(2 * m)])
    return [sum_over_chips(w, pairs[w], m) * factor for w in (0, 1)]


def body(inputs, grad_out, blocks_one, slots_one, blocks_two, slots_two):
    owners = blocks_one.shape[0]
    entries = blocks_one.shape[2]
    size = blocks_one.shape[-1]
    n, m = lax.axis_size("ch"), lax.axis_size("tok") // 2
    tokens, width = inputs.shape
    per_slice = width // size
    feat_blocks = per_slice * n
    hid_blocks = H // n // size
    w_one = blocks_one.reshape(owners * entries, size, size)
    w_two = blocks_two.reshape(owners * entries, size, size)
    slots = jnp.concatenate([slots_one, slots_two], axis=1)
    ints = lambda count: jax.ShapeDtypeStruct((count,), jnp.int32)
    mine = kernel_call(
        functools.partial(need_kernel, feat_blocks, hid_blocks),
        "needed_features",
        out_shape=ints(2),
        in_specs=[SMEM],
        out_specs=SMEM,
    )(slots)
    rows = jax.ShapeDtypeStruct((4, owners * entries + GROUP), jnp.int32)
    one, two = kernel_call(
        functools.partial(list_kernel, feat_blocks, hid_blocks),
        "list_entries",
        out_shape=[rows] * 2,
        in_specs=[SMEM],
        out_specs=[SMEM] * 2,
    )(slots)
    masks = [mine] + [lax.ppermute(mine, "ch", move) for move in rounds(n)]
    tok = lax.axis_index("tok")
    where = jnp.stack([lax.axis_index("ch"), tok % 2, tok // 2]).astype(jnp.int32)
    fetch_rows = room(FETCH_ROWS, n, 2 * per_slice)
    back_rows = room(BACK_ROWS, n, per_slice)
    meta, levels = kernel_call(
        functools.partial(plan_kernel, n, per_slice, fetch_rows, back_rows),
        "plan",
        out_shape=[ints(META_MASKS + 2 * n), ints(3)],
        in_specs=[SMEM] * (n + 1),
        out_specs=[SMEM] * 2,
    )(where, *masks)
    xs, dys = lax.switch(
        levels[0], [functools.partial(fetch_blocks, row, n, size) for row in fetch_rows], meta, inputs, grad_out
    )
    own, acts, pres, *backs = kernel_call(
        functools.partial(shard_kernel, n, per_slice, hid_blocks),
        "shard_blocks",
        out_shape=[
            floats(tokens, width),
            *[floats(hid_blocks, tokens, size)] * 2,
            *[pltpu.VMEM((per_slice, tokens, size), jnp.float32)] * (n - 1),
        ],
        in_specs=[SMEM] * 3 + [ANY] * 4,
        out_specs=[VMEM] + [ANY] * (n + 1),
        scratch_shapes=[
            pltpu.VMEM((feat_blocks, tokens, size), jnp.float32),
            pltpu.VMEM((feat_blocks, tokens, size), jnp.float32),
            pltpu.VMEM((feat_blocks + 1, tokens, size), jnp.float32),
            pltpu.VMEM((hid_blocks + 1, tokens, size), jnp.float32),
            pltpu.VMEM((hid_blocks + 1, tokens, size), jnp.float32),
            pltpu.VMEM(w_one.shape, jnp.float32),
            pltpu.VMEM(w_two.shape, jnp.float32),
            pltpu.SemaphoreType.DMA((2, feat_blocks)),
            pltpu.SemaphoreType.DMA((feat_blocks,)),
            pltpu.SemaphoreType.DMA((2,)),
            pltpu.SemaphoreType.DMA((2, hid_blocks)),
        ],
        flops=5 * 10**9,
        moved=16 * 2**20,
    )(meta, one, two, xs, dys, *kept_in(pltpu.HBM, w_one, w_two))
    factor = 1.0 / math.sqrt(inputs.shape[0] * lax.axis_size("tok"))
    grad_x, grad_one, grad_two = lax.switch(
        levels[1],
        [functools.partial(send_results, row, n, m, hid_blocks, entries, factor) for row in back_rows],
        levels[2],
        meta,
        one,
        two,
        xs,
        dys,
        acts,
        pres,
        own,
        *backs,
    )
    grad_one = grad_one.reshape(1, 1, entries, size, size)
    grad_two = grad_two.reshape(1, 1, entries, size, size)
    return (grad_x, grad_one, grad_two)


def solution(mesh):
    in_specs = (
        P("tok", "ch"),
        P("tok", "ch"),
        P(None, "ch", None, None, None),
        P(None, "ch", None),
        P(None, "ch", None, None, None),
        P(None, "ch", None),
    )
    out_specs = (P("tok", "ch"), P("tok", "ch", None, None, None), P("tok", "ch", None, None, None))
    return jax.shard_map(body, mesh=mesh, in_specs=in_specs, out_specs=out_specs, check_vma=False)
```

```python
import functools
import math

import jax
import jax.numpy as jnp
from jax import lax
from jax.experimental import pallas as pl
from jax.experimental.pallas import tpu as pltpu
from jax.sharding import PartitionSpec as P

H = 8192

VMEM_LIMIT = 36 * 2**20
ANY = pl.BlockSpec(memory_space=pl.ANY)
SMEM = pl.BlockSpec(memory_space=pltpu.SMEM)
VMEM = pl.BlockSpec(memory_space=pltpu.VMEM)
NN = (((1,), (0,)), ((), ()))
NT = (((1,), (1,)), ((), ()))
TN = (((0,), (0,)), ((), ()))

FETCH_ROWS = (
    (10, 6, 6),
    (11, 7, 6),
    (11, 6, 7),
    (12, 7, 7),
    (12, 8, 6),
    (13, 7, 8),
    (13, 6, 9),
    (14, 9, 7),
    (14, 8, 8),
    (15, 7, 10),
    (15, 10, 7),
    (16, 9, 9),
    (16, 8, 12),
    (16, 12, 8),
    (16, 11, 11),
    (16, 16, 16),
)
BACK_ROWS = (
    (6, 3, 4),
    (6, 4, 3),
    (7, 4, 4),
    (8, 4, 5),
    (8, 5, 4),
    (8, 5, 6),
    (8, 6, 5),
    (8, 8, 8),
)


def room(rows, n, most):
    bands = [0 if r < n // 2 else 1 + r % 2 for r in range(1, n)]
    full = max(max(row) for row in rows)
    sized = []
    for row in rows:
        caps = tuple(-(-row[b] * most // full) for b in bands)
        if caps not in sized:
            sized.append(caps)
    return sized


def split(value):
    high = value.astype(jnp.bfloat16)
    return high, (value - high.astype(jnp.float32)).astype(jnp.bfloat16)


def halves(value):
    return jnp.concatenate(split(value), axis=1)


def dot_wide(left, right, dims):
    return lax.dot_general(left, right, dims, preferred_element_type=jnp.float32)


def dot_nn(left, right):
    high, low = split(right)
    both = jnp.concatenate(
        [
            jnp.concatenate([high, low], axis=1),
            jnp.concatenate([high, jnp.zeros_like(low)], axis=1),
        ],
        axis=0,
    )
    out = dot_wide(halves(left), both, NN)
    size = right.shape[1]
    return out[:, :size] + out[:, size:]


def dot_nt(left, right):
    high, low = split(right)
    both = jnp.concatenate(
        [
            jnp.concatenate([high, high], axis=1),
            jnp.concatenate([low, jnp.zeros_like(low)], axis=1),
        ],
        axis=0,
    )
    out = dot_wide(halves(left), both, NT)
    size = right.shape[0]
    return out[:, :size] + out[:, size:]


def dot_tn(left, right):
    out = dot_wide(halves(left), halves(right), TN)
    rows, columns = left.shape[1], right.shape[1]
    return out[:rows, :columns] + (out[:rows, columns:] + out[rows:, :columns])


def bit_of(mask, place):
    return lax.shift_right_arithmetic(mask, place) & 1


def for_bits(mask, first, count, start, visit):
    def step(k, pos):
        bit = bit_of(mask, first + k)

        @pl.when(bit == 1)
        def _():
            visit(k, pos)

        return pos + bit

    return lax.fori_loop(0, count, step, start)


def lanes(block, size):
    return pl.ds(pl.multiple_of(block * size, size), size)


GROUP, PAIR = 4, 2
UNROLL = 8
META_ME, META_CORE, META_CHIP, META_MASKS = 0, 1, 2, 3


def pack_kernel(n, per_slice, meta, x, dy, *rest):
    sends, sem = rest[:-1], rest[-1]
    me = meta[META_ME]
    size = sends[0].shape[-1]

    def visit_all(act):
        for s in range(1, n):
            target = me ^ s
            pos = 0
            for a, source in enumerate((x, dy)):

                def visit(k, pos, a=a, source=source, s=s):
                    act(
                        pltpu.make_async_copy(
                            source.at[:, lanes(k, size)],
                            sends[s - 1].at[pos],
                            sem.at[s - 1, a * per_slice + k],
                        )
                    )

                pos = for_bits(meta[META_MASKS + 2 * target + a], me * per_slice, per_slice, pos, visit)

    visit_all(lambda copy: copy.start())
    visit_all(lambda copy: copy.wait())


def place_kernel(n, per_slice, meta, x, dy, *rest):
    recvs, targets, sem = rest[: n - 1], rest[n - 1 : n + 1], rest[n + 1]
    me = meta[META_ME]
    size = x.shape[-1] // per_slice

    def visit_all(act):
        for s in range(n):
            first = (me ^ s) * per_slice
            pos = 0
            for a, source in enumerate((x, dy)):

                def visit(k, pos, a=a, source=source, s=s, first=first):
                    block = source.at[:, lanes(k, size)] if s == 0 else recvs[s - 1].at[pos]
                    act(pltpu.make_async_copy(block, targets[a].at[first + k], sem.at[a, first + k]))

                pos = for_bits(meta[META_MASKS + 2 * me + a], first, per_slice, pos, visit)

    visit_all(lambda copy: copy.start())
    visit_all(lambda copy: copy.wait())


def load_needed(meta, sources, targets, sem, act, which=(0, 1)):
    for a in which:

        def visit(k, pos, a=a):
            act(pltpu.make_async_copy(sources[a].at[k], targets[a].at[k], sem.at[a, k]))

        for_bits(meta[META_MASKS + 2 * meta[META_ME] + a], 0, targets[a].shape[0], 0, visit)


def quotient(value, by):
    if by & (by - 1) == 0:
        return lax.shift_right_logical(value, by.bit_length() - 1), value & (by - 1)
    return lax.div(value, by), lax.rem(value, by)


def entries_of(slots):
    return slots.shape[0] * slots.shape[2]


def slot_of(slots, w, e):
    owner, c = quotient(e, slots.shape[2])
    return slots[owner, w, c]


def entry_one(slots, e, feat_blocks, hid_blocks):
    s = slot_of(slots, 0, e)
    f, h = quotient(s, hid_blocks)
    return s < feat_blocks * hid_blocks, f, h


def entry_two(slots, e, feat_blocks, hid_blocks):
    s = slot_of(slots, 1, e)
    h, f = quotient(s, feat_blocks)
    return s < feat_blocks * hid_blocks, f, h


def active_hidden(slots, feat_blocks, hid_blocks):
    def step(e, masks):
        found = []
        for mask, entry in zip(masks, (entry_one, entry_two)):
            live, _, h = entry(slots, e, feat_blocks, hid_blocks)
            found.append(mask | jnp.where(live, lax.shift_left(1, jnp.where(live, h, 0)), 0))
        return tuple(found)

    one, two = lax.fori_loop(0, entries_of(slots), step, (0, 0), unroll=UNROLL)
    return one & two


def need_kernel(feat_blocks, hid_blocks, slots, out):
    active = active_hidden(slots, feat_blocks, hid_blocks)

    def step(e, masks):
        found = []
        for mask, entry in zip(masks, (entry_one, entry_two)):
            live, f, h = entry(slots, e, feat_blocks, hid_blocks)
            wanted = live & (bit_of(active, jnp.where(live, h, 0)) == 1)
            found.append(mask | jnp.where(wanted, lax.shift_left(1, jnp.where(wanted, f, 0)), 0))
        return tuple(found)

    out[0], out[1] = lax.fori_loop(0, entries_of(slots), step, (0, 0), unroll=UNROLL)


def ones(mask):
    shift = lax.shift_right_logical
    pairs = mask - (shift(mask, 1) & 0x55555555)
    fours = (pairs & 0x33333333) + (shift(pairs, 2) & 0x33333333)
    eights = (fours + shift(fours, 4)) & 0x0F0F0F0F
    sixteens = eights + shift(eights, 8)
    return (sixteens + shift(sixteens, 16)) & 63


def plan_kernel(n, per_slice, fetch_rows, back_rows, where, *rest):
    masks, meta, levels = rest[:n], rest[n], rest[n + 1]
    needed = functools.reduce(lax.bitwise_or, [mask[0] for mask in masks])
    levels[2] = jnp.where(needed != 0, 1, 0)
    me = where[0]
    for k in range(3):
        meta[k] = where[k]
    for s in range(n):
        place = META_MASKS + 2 * (me ^ s)
        meta[place] = masks[s][0]
        meta[place + 1] = masks[s][1]
    low = (1 << per_slice) - 1
    most_fetch, most_back = [], []
    for s in range(1, n):

        def widest(i, most, s=s):
            place = META_MASKS + 2 * (i ^ s)
            counts = [ones(lax.shift_right_logical(meta[place + a], i * per_slice) & low) for a in (0, 1)]
            return jnp.maximum(most[0], counts[0] + counts[1]), jnp.maximum(most[1], counts[0])

        fetch, back = lax.fori_loop(0, n, widest, (0, 0))
        most_fetch.append(fetch)
        most_back.append(back)
    for k, (rows, most) in enumerate(((fetch_rows, most_fetch), (back_rows, most_back))):
        level = len(rows) - 1
        for r in range(len(rows) - 2, -1, -1):
            fits = most[0] <= rows[r][0]
            for s in range(1, n - 1):
                fits = fits & (most[s] <= rows[r][s])
            level = jnp.where(fits, r, level)
        levels[k] = level


def list_kernel(feat_blocks, hid_blocks, slots, one, two):
    active = active_hidden(slots, feat_blocks, hid_blocks)
    for entry, listed in ((entry_one, one), (entry_two, two)):

        def step(e, count, entry=entry, listed=listed):
            live, f, h = entry(slots, e, feat_blocks, hid_blocks)
            h = jnp.where(live, h, 0)
            for k, value in enumerate((e, jnp.where(live, f, 0), h)):
                listed[k, count] = value
            return count + jnp.where(live, bit_of(active, h), 0)

        count = lax.fori_loop(0, entries_of(slots), step, 0)
        for k in range(GROUP - 1):
            for row, value in enumerate((0, feat_blocks, hid_blocks)):
                listed[row, count + k] = value
        listed[3, 0] = count
        listed[3, 1] = active


def groups(count, group):
    return lax.div(count + (group - 1), group)


def shard_kernel(n, per_slice, hid_blocks, meta, one, two, x, dy, w_one, w_two, *rest):
    own_out, acts_out, pres_out = rest[:3]
    backs = rest[3 : n + 2]
    xs, dys, gxs, acts, pres, ones_in, twos_in, sem, back_sem, w_sem, hidden_sem = rest[n + 2 :]
    feat_blocks = xs.shape[0]
    me = meta[META_ME]
    size = xs.shape[-1]
    load = functools.partial(load_needed, meta, (x, dy), (xs, dys), sem)
    weights = [
        pltpu.make_async_copy(source, target, w_sem.at[k])
        for k, (source, target) in enumerate(((w_one, ones_in), (w_two, twos_in)))
    ]
    for a, copy in enumerate(weights):
        load(lambda copy: copy.start(), which=(a,))
        copy.start()
    count_one, count_two, active = one[3, 0], two[3, 0], one[3, 1]
    mask_x = meta[META_MASKS + 2 * me]

    def clear_hidden(h, pos):
        acts[h] = jnp.zeros(acts.shape[1:], jnp.float32)
        pres[h] = jnp.zeros(pres.shape[1:], jnp.float32)

    for_bits(active, 0, hid_blocks, 0, clear_hidden)

    def clear_feature(k, pos):
        gxs[k] = jnp.zeros(gxs.shape[1:], jnp.float32)

    for_bits(mask_x, 0, feat_blocks, 0, clear_feature)
    rows = 64

    def clear_own(k, carry):
        own_out[pl.ds(pl.multiple_of(rows * k, rows), rows)] = jnp.zeros((rows, own_out.shape[1]), jnp.float32)
        return carry

    lax.fori_loop(0, own_out.shape[0] // rows, clear_own, 0)


    def accumulate(listed, count, product, into, target):
        def step(g, carry):
            entries = [[listed[row, GROUP * g + k] for row in range(3)] for k in range(GROUP)]
            terms = [product(e, f, h) for e, f, h in entries]
            for entry, term in zip(entries, terms):
                into[entry[target]] += term
            return carry

        lax.fori_loop(0, groups(count, GROUP), step, 0)

    def ready(a):
        load(lambda copy: copy.wait(), which=(a,))
        weights[a].wait()

    last = feat_blocks - 1
    ready(0)
    accumulate(one, count_one, lambda e, f, h: dot_nn(xs[jnp.minimum(f, last)], ones_in[e]), acts, 2)
    ready(1)
    accumulate(two, count_two, lambda e, f, h: dot_nt(dys[jnp.minimum(f, last)], twos_in[e]), pres, 2)

    def gelu(h, pos):
        pre_act = acts[h]
        cdf = 0.5 * (1.0 + lax.erf(pre_act * (1.0 / math.sqrt(2.0))))
        pdf = jnp.exp(-0.5 * pre_act * pre_act) * (1.0 / math.sqrt(2.0 * math.pi))
        acts[h] = pre_act * cdf
        pres[h] = pres[h] * (cdf + pre_act * pdf)

    for_bits(active, 0, hid_blocks, 0, gelu)

    def hand_on(act):
        def visit(h, pos):
            for k, (source, target) in enumerate(((acts, acts_out), (pres, pres_out))):
                act(pltpu.make_async_copy(source.at[h], target.at[h], hidden_sem.at[k, h]))

        for_bits(active, 0, hid_blocks, 0, visit)

    hand_on(lambda copy: copy.start())
    accumulate(one, count_one, lambda e, f, h: dot_nt(pres[jnp.minimum(h, hid_blocks - 1)], ones_in[e]), gxs, 1)

    def send_back(act):
        for s in range(1, n):
            first = (me ^ s) * per_slice

            def visit(k, pos, s=s, first=first):
                act(pltpu.make_async_copy(gxs.at[first + k], backs[s - 1].at[pos], back_sem.at[first + k]))

            for_bits(mask_x, first, per_slice, 0, visit)

    send_back(lambda copy: copy.start())

    def keep(k, pos):
        own_out[:, lanes(k, size)] = gxs[me * per_slice + k]

    for_bits(mask_x, me * per_slice, per_slice, 0, keep)
    send_back(lambda copy: copy.wait())
    hand_on(lambda copy: copy.wait())


def blocks_kernel(hid_blocks, meta, one, two, x, dy, acts, pres, keep_out, send_out, xs, dys, sem):
    per_owner = keep_out.shape[2]
    core, chip = meta[META_CORE], meta[META_CHIP]
    count_one, count_two = one[3, 0], two[3, 0]
    load = functools.partial(load_needed, meta, (x, dy), (xs, dys), sem)
    load(lambda copy: copy.start())

    def clear_blocks(k, carry):
        w, chip_at = lax.div(k, keep_out.shape[1]), lax.rem(k, keep_out.shape[1])
        for out in (keep_out, send_out):
            out[w, chip_at] = jnp.zeros(out.shape[2:], jnp.float32)
        return carry

    lax.fori_loop(0, 2 * keep_out.shape[1], clear_blocks, 0)
    load(lambda copy: copy.wait())

    def fill(w, listed, count, product):
        def step(g, carry):
            places = [jnp.minimum(PAIR * g + k, count - 1) for k in range(PAIR)]
            entries = [[listed[row, place] for row in range(3)] for place in places]
            terms = [product(f, h) for _, f, h in entries]
            for (e, _, _), term in zip(entries, terms):
                owner, c = lax.div(e, per_owner), lax.rem(e, per_owner)
                where = lax.div(owner, 2) ^ chip
                mine = lax.rem(owner, 2) == core

                @pl.when(mine)
                def _(where=where, c=c, term=term):
                    keep_out[w, where, c] = term

                @pl.when(jnp.logical_not(mine))
                def _(where=where, c=c, term=term):
                    send_out[w, where, c] = term

            return carry

        lax.fori_loop(0, groups(count, PAIR), step, 0)

    fill(0, one, count_one, lambda f, h: dot_tn(xs[f], pres[h]))
    fill(1, two, count_two, lambda f, h: dot_tn(acts[h], dys[f]))


def add_kernel(n, per_slice, meta, own, *rest):
    recvs, out, landed, sem = rest[: n - 1], rest[n - 1], rest[n], rest[n + 1]
    me = meta[META_ME]
    size = landed.shape[-1]

    def visit_all(visit):
        for s in range(1, n):
            mask = meta[META_MASKS + 2 * (me ^ s)]
            for_bits(mask, me * per_slice, per_slice, 0, functools.partial(visit, s - 1))

    def copy(place, k, pos):
        return pltpu.make_async_copy(recvs[place].at[pos], landed.at[place, k], sem.at[place, k])

    visit_all(lambda place, k, pos: copy(place, k, pos).start())
    out[...] = own[...]

    def add(place, k, pos):
        copy(place, k, pos).wait()
        out[:, lanes(k, size)] += landed[place, k]

    visit_all(add)


def kernel_call(kernel, name, *, out_shape, in_specs, out_specs, scratch_shapes=(), flops=0, moved=0):
    return pl.pallas_call(
        kernel,
        out_shape=out_shape,
        in_specs=in_specs,
        out_specs=out_specs,
        scratch_shapes=scratch_shapes,
        compiler_params=pltpu.CompilerParams(vmem_limit_bytes=VMEM_LIMIT),
        cost_estimate=pl.CostEstimate(flops=flops, bytes_accessed=moved, transcendentals=0),
        name=name,
    )


def kept_in(space, *arrays):
    return [pltpu.with_memory_space_constraint(array, space) for array in arrays]


def floats(*dims):
    return jax.ShapeDtypeStruct(dims, jnp.float32)


def rounds(n):
    return [[(k, k ^ r) for k in range(n)] for r in range(1, n)]


def fetch_blocks(caps, n, size, meta, x, dy):
    tokens, width = x.shape
    per_slice = width // size
    sends = kernel_call(
        functools.partial(pack_kernel, n, per_slice),
        "pack_blocks",
        out_shape=[pltpu.VMEM((cap, tokens, size), jnp.float32) for cap in caps],
        in_specs=[SMEM, ANY, ANY],
        out_specs=[ANY] * (n - 1),
        scratch_shapes=[pltpu.SemaphoreType.DMA((n - 1, 2 * per_slice))],
        moved=2 * 2**20,
    )(meta, *kept_in(pltpu.HBM, x, dy))
    recvs = [lax.ppermute(s, "ch", move) for s, move in zip(sends, rounds(n))]
    return kernel_call(
        functools.partial(place_kernel, n, per_slice),
        "place_blocks",
        out_shape=[floats(n * per_slice, tokens, size)] * 2,
        in_specs=[SMEM, VMEM, VMEM] + [ANY] * (n - 1),
        out_specs=[ANY] * 2,
        scratch_shapes=[pltpu.SemaphoreType.DMA((2, n * per_slice))],
        moved=2 * 2**20,
    )(meta, x, dy, *kept_in(pltpu.VMEM, *recvs))


def sum_over_chips(w, mine, m):
    steps = m.bit_length() - 1
    order = range(steps) if w == 0 else range(steps - 1, -1, -1)
    whole = mine.reshape((2,) * steps + mine.shape[1:])
    for k in order:
        axis = steps - 1 - k
        keep = lax.index_in_dim(whole, 0, axis, keepdims=True)
        send = lax.index_in_dim(whole, 1, axis, keepdims=True)
        whole = keep + lax.ppermute(send, "tok", [(t, t ^ (2 << k)) for t in range(2 * m)])
    return whole.reshape(mine.shape[1:])


def send_results(caps, n, m, hid_blocks, per_owner, factor, any_needed, meta, one, two, xs, dys, acts, pres, own, *backs):
    tokens, width = own.shape
    size = xs.shape[-1]
    per_slice = width // size
    came = [lax.ppermute(b[:cap], "ch", move) for b, cap, move in zip(backs, caps, rounds(n))]
    grad_x = kernel_call(
        functools.partial(add_kernel, n, per_slice),
        "add_back",
        out_shape=floats(tokens, per_slice * size),
        in_specs=[SMEM, VMEM] + [ANY] * (n - 1),
        out_specs=VMEM,
        scratch_shapes=[
            pltpu.VMEM((n - 1, per_slice, tokens, size), jnp.float32),
            pltpu.SemaphoreType.DMA((n - 1, per_slice)),
        ],
    )(meta, own, *came)
    sums = lax.cond(
        any_needed > 0,
        functools.partial(gradient_blocks, m, hid_blocks, per_owner, factor),
        lambda *operands: [jnp.zeros((per_owner, size, size), own.dtype)] * 2,
        meta,
        one,
        two,
        xs,
        dys,
        acts,
        pres,
    )
    return grad_x, *sums


def gradient_blocks(m, hid_blocks, per_owner, factor, meta, one, two, xs, dys, acts, pres):
    feat_blocks, _, size = xs.shape
    keep, send = kernel_call(
        functools.partial(blocks_kernel, hid_blocks),
        "gradient_blocks",
        out_shape=[floats(2, m, per_owner, size, size)] * 2,
        in_specs=[SMEM] * 3 + [ANY] * 2 + [VMEM] * 2,
        out_specs=[VMEM] * 2,
        scratch_shapes=[
            pltpu.VMEM(xs.shape, jnp.float32),
            pltpu.VMEM(xs.shape, jnp.float32),
            pltpu.SemaphoreType.DMA((2, feat_blocks)),
        ],
        flops=2 * 10**9,
        moved=16 * 2**20,
    )(meta, one, two, xs, dys, acts, pres)
    return sum_over_tokens(m, factor, keep, send)


def sum_over_tokens(m, factor, keep, send):
    pairs = keep + lax.ppermute(send, "tok", [(t, t ^ 1) for t in range(2 * m)])
    return [sum_over_chips(w, pairs[w], m) * factor for w in (0, 1)]


def body(inputs, grad_out, blocks_one, slots_one, blocks_two, slots_two):
    owners = blocks_one.shape[0]
    entries = blocks_one.shape[2]
    size = blocks_one.shape[-1]
    n, m = lax.axis_size("ch"), lax.axis_size("tok") // 2
    tokens, width = inputs.shape
    per_slice = width // size
    feat_blocks = per_slice * n
    hid_blocks = H // n // size
    w_one = blocks_one.reshape(owners * entries, size, size)
    w_two = blocks_two.reshape(owners * entries, size, size)
    slots = jnp.concatenate([slots_one, slots_two], axis=1)
    ints = lambda count: jax.ShapeDtypeStruct((count,), jnp.int32)
    mine = kernel_call(
        functools.partial(need_kernel, feat_blocks, hid_blocks),
        "needed_features",
        out_shape=ints(2),
        in_specs=[SMEM],
        out_specs=SMEM,
    )(slots)
    rows = jax.ShapeDtypeStruct((4, owners * entries + GROUP), jnp.int32)
    one, two = kernel_call(
        functools.partial(list_kernel, feat_blocks, hid_blocks),
        "list_entries",
        out_shape=[rows] * 2,
        in_specs=[SMEM],
        out_specs=[SMEM] * 2,
    )(slots)
    masks = [mine] + [lax.ppermute(mine, "ch", move) for move in rounds(n)]
    tok = lax.axis_index("tok")
    where = jnp.stack([lax.axis_index("ch"), tok % 2, tok // 2]).astype(jnp.int32)
    fetch_rows = room(FETCH_ROWS, n, 2 * per_slice)
    back_rows = room(BACK_ROWS, n, per_slice)
    meta, levels = kernel_call(
        functools.partial(plan_kernel, n, per_slice, fetch_rows, back_rows),
        "plan",
        out_shape=[ints(META_MASKS + 2 * n), ints(3)],
        in_specs=[SMEM] * (n + 1),
        out_specs=[SMEM] * 2,
    )(where, *masks)
    xs, dys = lax.switch(
        levels[0], [functools.partial(fetch_blocks, row, n, size) for row in fetch_rows], meta, inputs, grad_out
    )
    own, acts, pres, *backs = kernel_call(
        functools.partial(shard_kernel, n, per_slice, hid_blocks),
        "shard_blocks",
        out_shape=[
            floats(tokens, width),
            *[floats(hid_blocks, tokens, size)] * 2,
            *[pltpu.VMEM((per_slice, tokens, size), jnp.float32)] * (n - 1),
        ],
        in_specs=[SMEM] * 3 + [ANY] * 4,
        out_specs=[VMEM] + [ANY] * (n + 1),
        scratch_shapes=[
            pltpu.VMEM((feat_blocks, tokens, size), jnp.float32),
            pltpu.VMEM((feat_blocks, tokens, size), jnp.float32),
            pltpu.VMEM((feat_blocks + 1, tokens, size), jnp.float32),
            pltpu.VMEM((hid_blocks + 1, tokens, size), jnp.float32),
            pltpu.VMEM((hid_blocks + 1, tokens, size), jnp.float32),
            pltpu.VMEM(w_one.shape, jnp.float32),
            pltpu.VMEM(w_two.shape, jnp.float32),
            pltpu.SemaphoreType.DMA((2, feat_blocks)),
            pltpu.SemaphoreType.DMA((feat_blocks,)),
            pltpu.SemaphoreType.DMA((2,)),
            pltpu.SemaphoreType.DMA((2, hid_blocks)),
        ],
        flops=5 * 10**9,
        moved=16 * 2**20,
    )(meta, one, two, xs, dys, *kept_in(pltpu.HBM, w_one, w_two))
    factor = 1.0 / math.sqrt(inputs.shape[0] * lax.axis_size("tok"))
    grad_x, grad_one, grad_two = lax.switch(
        levels[1],
        [functools.partial(send_results, row, n, m, hid_blocks, entries, factor) for row in back_rows],
        levels[2],
        meta,
        one,
        two,
        xs,
        dys,
        acts,
        pres,
        own,
        *backs,
    )
    grad_one = grad_one.reshape(1, 1, entries, size, size)
    grad_two = grad_two.reshape(1, 1, entries, size, size)
    return (grad_x, grad_one, grad_two)


def solution(mesh):
    in_specs = (
        P("tok", "ch"),
        P("tok", "ch"),
        P(None, "ch", None, None, None),
        P(None, "ch", None),
        P(None, "ch", None, None, None),
        P(None, "ch", None),
    )
    out_specs = (P("tok", "ch"), P("tok", "ch", None, None, None), P("tok", "ch", None, None, None))
    return jax.shard_map(body, mesh=mesh, in_specs=in_specs, out_specs=out_specs, check_vma=False)
```

```python
import functools
import math

import jax
import jax.numpy as jnp
from jax import lax
from jax.experimental import pallas as pl
from jax.experimental.pallas import tpu as pltpu
from jax.sharding import PartitionSpec as P

H = 8192

VMEM_LIMIT = 36 * 2**20
ANY = pl.BlockSpec(memory_space=pl.ANY)
SMEM = pl.BlockSpec(memory_space=pltpu.SMEM)
VMEM = pl.BlockSpec(memory_space=pltpu.VMEM)
NN = (((1,), (0,)), ((), ()))
NT = (((1,), (1,)), ((), ()))
TN = (((0,), (0,)), ((), ()))

FETCH_ROWS = (
    (10, 6, 6),
    (11, 7, 6),
    (11, 6, 7),
    (12, 7, 7),
    (12, 8, 6),
    (13, 7, 8),
    (13, 6, 9),
    (14, 9, 7),
    (14, 8, 8),
    (15, 7, 10),
    (15, 10, 7),
    (16, 9, 9),
    (16, 8, 12),
    (16, 12, 8),
    (16, 11, 11),
    (16, 16, 16),
)
BACK_ROWS = (
    (6, 3, 4),
    (6, 4, 3),
    (7, 4, 4),
    (8, 4, 5),
    (8, 5, 4),
    (8, 5, 6),
    (8, 6, 5),
    (8, 8, 8),
)


def room(rows, n, most):
    bands = [0 if r < n // 2 else 1 + r % 2 for r in range(1, n)]
    full = max(max(row) for row in rows)
    sized = []
    for row in rows:
        caps = tuple(-(-row[b] * most // full) for b in bands)
        if caps not in sized:
            sized.append(caps)
    return sized


def split(value):
    high = value.astype(jnp.bfloat16)
    return high, (value - high.astype(jnp.float32)).astype(jnp.bfloat16)


def halves(value):
    return jnp.concatenate(split(value), axis=1)


def dot_wide(left, right, dims):
    return lax.dot_general(left, right, dims, preferred_element_type=jnp.float32)


def dot_nn(left, right):
    high, low = split(right)
    both = jnp.concatenate(
        [
            jnp.concatenate([high, low], axis=1),
            jnp.concatenate([high, jnp.zeros_like(low)], axis=1),
        ],
        axis=0,
    )
    out = dot_wide(halves(left), both, NN)
    size = right.shape[1]
    return out[:, :size] + out[:, size:]


def dot_nt(left, right):
    high, low = split(right)
    both = jnp.concatenate(
        [
            jnp.concatenate([high, high], axis=1),
            jnp.concatenate([low, jnp.zeros_like(low)], axis=1),
        ],
        axis=0,
    )
    out = dot_wide(halves(left), both, NT)
    size = right.shape[0]
    return out[:, :size] + out[:, size:]


def dot_tn(left, right):
    out = dot_wide(halves(left), halves(right), TN)
    rows, columns = left.shape[1], right.shape[1]
    return out[:rows, :columns] + (out[:rows, columns:] + out[rows:, :columns])


def bit_of(mask, place):
    return lax.shift_right_arithmetic(mask, place) & 1


def for_bits(mask, first, count, start, visit):
    def step(k, pos):
        bit = bit_of(mask, first + k)

        @pl.when(bit == 1)
        def _():
            visit(k, pos)

        return pos + bit

    return lax.fori_loop(0, count, step, start)


def lanes(block, size):
    return pl.ds(pl.multiple_of(block * size, size), size)


GROUP, PAIR = 4, 2
UNROLL = 8
META_ME, META_CORE, META_CHIP, META_MASKS = 0, 1, 2, 3


def pack_kernel(n, per_slice, meta, x, dy, *rest):
    sends, sem = rest[:-1], rest[-1]
    me = meta[META_ME]
    size = sends[0].shape[-1]

    def visit_all(act):
        for s in range(1, n):
            target = me ^ s
            pos = 0
            for a, source in enumerate((x, dy)):

                def visit(k, pos, a=a, source=source, s=s):
                    act(
                        pltpu.make_async_copy(
                            source.at[:, lanes(k, size)],
                            sends[s - 1].at[pos],
                            sem.at[s - 1, a * per_slice + k],
                        )
                    )

                pos = for_bits(meta[META_MASKS + 2 * target + a], me * per_slice, per_slice, pos, visit)

    visit_all(lambda copy: copy.start())
    visit_all(lambda copy: copy.wait())


def place_kernel(n, per_slice, meta, x, dy, *rest):
    recvs, targets, sem = rest[: n - 1], rest[n - 1 : n + 1], rest[n + 1]
    me = meta[META_ME]
    size = x.shape[-1] // per_slice

    def visit_all(act):
        for s in range(n):
            first = (me ^ s) * per_slice
            pos = 0
            for a, source in enumerate((x, dy)):

                def visit(k, pos, a=a, source=source, s=s, first=first):
                    block = source.at[:, lanes(k, size)] if s == 0 else recvs[s - 1].at[pos]
                    act(pltpu.make_async_copy(block, targets[a].at[first + k], sem.at[a, first + k]))

                pos = for_bits(meta[META_MASKS + 2 * me + a], first, per_slice, pos, visit)

    visit_all(lambda copy: copy.start())
    visit_all(lambda copy: copy.wait())


def load_needed(meta, sources, targets, sem, act, which=(0, 1)):
    for a in which:

        def visit(k, pos, a=a):
            act(pltpu.make_async_copy(sources[a].at[k], targets[a].at[k], sem.at[a, k]))

        for_bits(meta[META_MASKS + 2 * meta[META_ME] + a], 0, targets[a].shape[0], 0, visit)


def quotient(value, by):
    if by & (by - 1) == 0:
        return lax.shift_right_logical(value, by.bit_length() - 1), value & (by - 1)
    return lax.div(value, by), lax.rem(value, by)


def entries_of(slots):
    return slots.shape[0] * slots.shape[2]


def slot_of(slots, w, e):
    owner, c = quotient(e, slots.shape[2])
    return slots[owner, w, c]


def entry_one(slots, e, feat_blocks, hid_blocks):
    s = slot_of(slots, 0, e)
    f, h = quotient(s, hid_blocks)
    return s < feat_blocks * hid_blocks, f, h


def entry_two(slots, e, feat_blocks, hid_blocks):
    s = slot_of(slots, 1, e)
    h, f = quotient(s, feat_blocks)
    return s < feat_blocks * hid_blocks, f, h


def active_hidden(slots, feat_blocks, hid_blocks):
    def step(e, masks):
        found = []
        for mask, entry in zip(masks, (entry_one, entry_two)):
            live, _, h = entry(slots, e, feat_blocks, hid_blocks)
            found.append(mask | jnp.where(live, lax.shift_left(1, jnp.where(live, h, 0)), 0))
        return tuple(found)

    one, two = lax.fori_loop(0, entries_of(slots), step, (0, 0), unroll=UNROLL)
    return one & two


def need_kernel(feat_blocks, hid_blocks, slots, out):
    active = active_hidden(slots, feat_blocks, hid_blocks)

    def step(e, masks):
        found = []
        for mask, entry in zip(masks, (entry_one, entry_two)):
            live, f, h = entry(slots, e, feat_blocks, hid_blocks)
            wanted = live & (bit_of(active, jnp.where(live, h, 0)) == 1)
            found.append(mask | jnp.where(wanted, lax.shift_left(1, jnp.where(wanted, f, 0)), 0))
        return tuple(found)

    out[0], out[1] = lax.fori_loop(0, entries_of(slots), step, (0, 0), unroll=UNROLL)


def ones(mask):
    shift = lax.shift_right_logical
    pairs = mask - (shift(mask, 1) & 0x55555555)
    fours = (pairs & 0x33333333) + (shift(pairs, 2) & 0x33333333)
    eights = (fours + shift(fours, 4)) & 0x0F0F0F0F
    sixteens = eights + shift(eights, 8)
    return (sixteens + shift(sixteens, 16)) & 63


def plan_kernel(n, per_slice, fetch_rows, back_rows, where, *rest):
    masks, meta, levels = rest[:n], rest[n], rest[n + 1]
    needed = functools.reduce(lax.bitwise_or, [mask[0] for mask in masks])
    levels[2] = jnp.where(needed != 0, 1, 0)
    me = where[0]
    for k in range(3):
        meta[k] = where[k]
    for s in range(n):
        place = META_MASKS + 2 * (me ^ s)
        meta[place] = masks[s][0]
        meta[place + 1] = masks[s][1]
    low = (1 << per_slice) - 1
    most_fetch, most_back = [], []
    for s in range(1, n):

        def widest(i, most, s=s):
            place = META_MASKS + 2 * (i ^ s)
            counts = [ones(lax.shift_right_logical(meta[place + a], i * per_slice) & low) for a in (0, 1)]
            return jnp.maximum(most[0], counts[0] + counts[1]), jnp.maximum(most[1], counts[0])

        fetch, back = lax.fori_loop(0, n, widest, (0, 0))
        most_fetch.append(fetch)
        most_back.append(back)
    for k, (rows, most) in enumerate(((fetch_rows, most_fetch), (back_rows, most_back))):
        level = len(rows) - 1
        for r in range(len(rows) - 2, -1, -1):
            fits = most[0] <= rows[r][0]
            for s in range(1, n - 1):
                fits = fits & (most[s] <= rows[r][s])
            level = jnp.where(fits, r, level)
        levels[k] = level


def list_kernel(feat_blocks, hid_blocks, slots, one, two):
    active = active_hidden(slots, feat_blocks, hid_blocks)
    for entry, listed in ((entry_one, one), (entry_two, two)):

        def step(e, count, entry=entry, listed=listed):
            live, f, h = entry(slots, e, feat_blocks, hid_blocks)
            h = jnp.where(live, h, 0)
            for k, value in enumerate((e, jnp.where(live, f, 0), h)):
                listed[k, count] = value
            return count + jnp.where(live, bit_of(active, h), 0)

        count = lax.fori_loop(0, entries_of(slots), step, 0)
        for k in range(GROUP - 1):
            for row, value in enumerate((0, feat_blocks, hid_blocks)):
                listed[row, count + k] = value
        listed[3, 0] = count
        listed[3, 1] = active


def groups(count, group):
    return lax.div(count + (group - 1), group)


def shard_kernel(n, per_slice, hid_blocks, meta, one, two, x, dy, w_one, w_two, *rest):
    own_out, acts_out, pres_out = rest[:3]
    backs = rest[3 : n + 2]
    xs, dys, gxs, acts, pres, ones_in, twos_in, sem, back_sem, w_sem, hidden_sem = rest[n + 2 :]
    feat_blocks = xs.shape[0]
    me = meta[META_ME]
    size = xs.shape[-1]
    load = functools.partial(load_needed, meta, (x, dy), (xs, dys), sem)
    weights = [
        pltpu.make_async_copy(source, target, w_sem.at[k])
        for k, (source, target) in enumerate(((w_one, ones_in), (w_two, twos_in)))
    ]
    for a, copy in enumerate(weights):
        load(lambda copy: copy.start(), which=(a,))
        copy.start()
    count_one, count_two, active = one[3, 0], two[3, 0], one[3, 1]
    mask_x = meta[META_MASKS + 2 * me]

    def clear_hidden(h, pos):
        acts[h] = jnp.zeros(acts.shape[1:], jnp.float32)
        pres[h] = jnp.zeros(pres.shape[1:], jnp.float32)

    for_bits(active, 0, hid_blocks, 0, clear_hidden)

    def clear_feature(k, pos):
        gxs[k] = jnp.zeros(gxs.shape[1:], jnp.float32)

    for_bits(mask_x, 0, feat_blocks, 0, clear_feature)
    rows = 64

    def clear_own(k, carry):
        own_out[pl.ds(pl.multiple_of(rows * k, rows), rows)] = jnp.zeros((rows, own_out.shape[1]), jnp.float32)
        return carry

    lax.fori_loop(0, own_out.shape[0] // rows, clear_own, 0)


    def accumulate(listed, count, product, into, target):
        def step(g, carry):
            entries = [[listed[row, GROUP * g + k] for row in range(3)] for k in range(GROUP)]
            terms = [product(e, f, h) for e, f, h in entries]
            for entry, term in zip(entries, terms):
                into[entry[target]] += term
            return carry

        lax.fori_loop(0, groups(count, GROUP), step, 0)

    def ready(a):
        load(lambda copy: copy.wait(), which=(a,))
        weights[a].wait()

    last = feat_blocks - 1
    ready(0)
    accumulate(one, count_one, lambda e, f, h: dot_nn(xs[jnp.minimum(f, last)], ones_in[e]), acts, 2)
    ready(1)
    accumulate(two, count_two, lambda e, f, h: dot_nt(dys[jnp.minimum(f, last)], twos_in[e]), pres, 2)

    def gelu(h, pos):
        pre_act = acts[h]
        cdf = 0.5 * (1.0 + lax.erf(pre_act * (1.0 / math.sqrt(2.0))))
        pdf = jnp.exp(-0.5 * pre_act * pre_act) * (1.0 / math.sqrt(2.0 * math.pi))
        acts[h] = pre_act * cdf
        pres[h] = pres[h] * (cdf + pre_act * pdf)

    for_bits(active, 0, hid_blocks, 0, gelu)

    def hand_on(act):
        def visit(h, pos):
            for k, (source, target) in enumerate(((acts, acts_out), (pres, pres_out))):
                act(pltpu.make_async_copy(source.at[h], target.at[h], hidden_sem.at[k, h]))

        for_bits(active, 0, hid_blocks, 0, visit)

    hand_on(lambda copy: copy.start())
    accumulate(one, count_one, lambda e, f, h: dot_nt(pres[jnp.minimum(h, hid_blocks - 1)], ones_in[e]), gxs, 1)

    def send_back(act):
        for s in range(1, n):
            first = (me ^ s) * per_slice

            def visit(k, pos, s=s, first=first):
                act(pltpu.make_async_copy(gxs.at[first + k], backs[s - 1].at[pos], back_sem.at[first + k]))

            for_bits(mask_x, first, per_slice, 0, visit)

    send_back(lambda copy: copy.start())

    def keep(k, pos):
        own_out[:, lanes(k, size)] = gxs[me * per_slice + k]

    for_bits(mask_x, me * per_slice, per_slice, 0, keep)
    send_back(lambda copy: copy.wait())
    hand_on(lambda copy: copy.wait())


def blocks_kernel(
    hid_blocks, meta, one, two, x, dy, acts_in, pres_in, keep_out, send_out, xs, dys, acts, pres, sem, hidden_sem
):
    per_owner = keep_out.shape[2]
    core, chip = meta[META_CORE], meta[META_CHIP]
    count_one, count_two = one[3, 0], two[3, 0]
    load = functools.partial(load_needed, meta, (x, dy), (xs, dys), sem)
    hidden = ((pres_in, pres), (acts_in, acts))

    def load_hidden(w, act):
        source, target = hidden[w]

        def visit(h, pos):
            act(pltpu.make_async_copy(source.at[h], target.at[h], hidden_sem.at[w, h]))

        for_bits(one[3, 1], 0, hid_blocks, 0, visit)

    for w in (0, 1):
        load(lambda copy: copy.start(), which=(w,))
        load_hidden(w, lambda copy: copy.start())

    def clear_blocks(k, carry):
        w, chip_at = lax.div(k, keep_out.shape[1]), lax.rem(k, keep_out.shape[1])
        for out in (keep_out, send_out):
            out[w, chip_at] = jnp.zeros(out.shape[2:], jnp.float32)
        return carry

    lax.fori_loop(0, 2 * keep_out.shape[1], clear_blocks, 0)

    def ready(w):
        load(lambda copy: copy.wait(), which=(w,))
        load_hidden(w, lambda copy: copy.wait())

    def fill(w, listed, count, product):
        def step(g, carry):
            places = [jnp.minimum(PAIR * g + k, count - 1) for k in range(PAIR)]
            entries = [[listed[row, place] for row in range(3)] for place in places]
            terms = [product(f, h) for _, f, h in entries]
            for (e, _, _), term in zip(entries, terms):
                owner, c = lax.div(e, per_owner), lax.rem(e, per_owner)
                where = lax.div(owner, 2) ^ chip
                mine = lax.rem(owner, 2) == core

                @pl.when(mine)
                def _(where=where, c=c, term=term):
                    keep_out[w, where, c] = term

                @pl.when(jnp.logical_not(mine))
                def _(where=where, c=c, term=term):
                    send_out[w, where, c] = term

            return carry

        lax.fori_loop(0, groups(count, PAIR), step, 0)

    ready(0)
    fill(0, one, count_one, lambda f, h: dot_tn(xs[f], pres[h]))
    ready(1)
    fill(1, two, count_two, lambda f, h: dot_tn(acts[h], dys[f]))


def add_kernel(n, per_slice, meta, own, *rest):
    recvs, out, landed, sem = rest[: n - 1], rest[n - 1], rest[n], rest[n + 1]
    me = meta[META_ME]
    size = landed.shape[-1]

    def visit_all(visit):
        for s in range(1, n):
            mask = meta[META_MASKS + 2 * (me ^ s)]
            for_bits(mask, me * per_slice, per_slice, 0, functools.partial(visit, s - 1))

    def copy(place, k, pos):
        return pltpu.make_async_copy(recvs[place].at[pos], landed.at[place, k], sem.at[place, k])

    visit_all(lambda place, k, pos: copy(place, k, pos).start())
    out[...] = own[...]

    def add(place, k, pos):
        copy(place, k, pos).wait()
        out[:, lanes(k, size)] += landed[place, k]

    visit_all(add)


def kernel_call(kernel, name, *, out_shape, in_specs, out_specs, scratch_shapes=(), flops=0, moved=0):
    return pl.pallas_call(
        kernel,
        out_shape=out_shape,
        in_specs=in_specs,
        out_specs=out_specs,
        scratch_shapes=scratch_shapes,
        compiler_params=pltpu.CompilerParams(vmem_limit_bytes=VMEM_LIMIT),
        cost_estimate=pl.CostEstimate(flops=flops, bytes_accessed=moved, transcendentals=0),
        name=name,
    )


def kept_in(space, *arrays):
    return [pltpu.with_memory_space_constraint(array, space) for array in arrays]


def floats(*dims):
    return jax.ShapeDtypeStruct(dims, jnp.float32)


def rounds(n):
    return [[(k, k ^ r) for k in range(n)] for r in range(1, n)]


def fetch_blocks(caps, n, size, meta, x, dy):
    tokens, width = x.shape
    per_slice = width // size
    sends = kernel_call(
        functools.partial(pack_kernel, n, per_slice),
        "pack_blocks",
        out_shape=[pltpu.VMEM((cap, tokens, size), jnp.float32) for cap in caps],
        in_specs=[SMEM, ANY, ANY],
        out_specs=[ANY] * (n - 1),
        scratch_shapes=[pltpu.SemaphoreType.DMA((n - 1, 2 * per_slice))],
        moved=2 * 2**20,
    )(meta, *kept_in(pltpu.HBM, x, dy))
    recvs = [lax.ppermute(s, "ch", move) for s, move in zip(sends, rounds(n))]
    return kernel_call(
        functools.partial(place_kernel, n, per_slice),
        "place_blocks",
        out_shape=[floats(n * per_slice, tokens, size)] * 2,
        in_specs=[SMEM, VMEM, VMEM] + [ANY] * (n - 1),
        out_specs=[ANY] * 2,
        scratch_shapes=[pltpu.SemaphoreType.DMA((2, n * per_slice))],
        moved=2 * 2**20,
    )(meta, x, dy, *kept_in(pltpu.VMEM, *recvs))


def sum_over_chips(w, mine, m):
    steps = m.bit_length() - 1
    order = range(steps) if w == 0 else range(steps - 1, -1, -1)
    whole = mine.reshape((2,) * steps + mine.shape[1:])
    for k in order:
        axis = steps - 1 - k
        keep = lax.index_in_dim(whole, 0, axis, keepdims=True)
        send = lax.index_in_dim(whole, 1, axis, keepdims=True)
        whole = keep + lax.ppermute(send, "tok", [(t, t ^ (2 << k)) for t in range(2 * m)])
    return whole.reshape(mine.shape[1:])


def send_results(caps, n, m, hid_blocks, per_owner, factor, any_needed, meta, one, two, xs, dys, acts, pres, own, *backs):
    tokens, width = own.shape
    size = xs.shape[-1]
    per_slice = width // size
    came = [lax.ppermute(b[:cap], "ch", move) for b, cap, move in zip(backs, caps, rounds(n))]
    grad_x = kernel_call(
        functools.partial(add_kernel, n, per_slice),
        "add_back",
        out_shape=floats(tokens, per_slice * size),
        in_specs=[SMEM, VMEM] + [ANY] * (n - 1),
        out_specs=VMEM,
        scratch_shapes=[
            pltpu.VMEM((n - 1, per_slice, tokens, size), jnp.float32),
            pltpu.SemaphoreType.DMA((n - 1, per_slice)),
        ],
    )(meta, own, *came)
    sums = lax.cond(
        any_needed > 0,
        functools.partial(gradient_blocks, m, hid_blocks, per_owner, factor),
        lambda *operands: [jnp.zeros((per_owner, size, size), own.dtype)] * 2,
        meta,
        one,
        two,
        xs,
        dys,
        acts,
        pres,
    )
    return grad_x, *sums


def gradient_blocks(m, hid_blocks, per_owner, factor, meta, one, two, xs, dys, acts, pres):
    feat_blocks, _, size = xs.shape
    keep, send = kernel_call(
        functools.partial(blocks_kernel, hid_blocks),
        "gradient_blocks",
        out_shape=[floats(2, m, per_owner, size, size)] * 2,
        in_specs=[SMEM] * 3 + [ANY] * 4,
        out_specs=[VMEM] * 2,
        scratch_shapes=[
            pltpu.VMEM(xs.shape, jnp.float32),
            pltpu.VMEM(xs.shape, jnp.float32),
            pltpu.VMEM(acts.shape, jnp.float32),
            pltpu.VMEM(pres.shape, jnp.float32),
            pltpu.SemaphoreType.DMA((2, feat_blocks)),
            pltpu.SemaphoreType.DMA((2, hid_blocks)),
        ],
        flops=2 * 10**9,
        moved=16 * 2**20,
    )(meta, one, two, xs, dys, acts, pres)
    return sum_over_tokens(m, factor, keep, send)


def sum_over_tokens(m, factor, keep, send):
    pairs = keep + lax.ppermute(send, "tok", [(t, t ^ 1) for t in range(2 * m)])
    return [sum_over_chips(w, pairs[w], m) * factor for w in (0, 1)]


def body(inputs, grad_out, blocks_one, slots_one, blocks_two, slots_two):
    owners = blocks_one.shape[0]
    entries = blocks_one.shape[2]
    size = blocks_one.shape[-1]
    n, m = lax.axis_size("ch"), lax.axis_size("tok") // 2
    tokens, width = inputs.shape
    per_slice = width // size
    feat_blocks = per_slice * n
    hid_blocks = H // n // size
    w_one = blocks_one.reshape(owners * entries, size, size)
    w_two = blocks_two.reshape(owners * entries, size, size)
    slots = jnp.concatenate([slots_one, slots_two], axis=1)
    ints = lambda count: jax.ShapeDtypeStruct((count,), jnp.int32)
    mine = kernel_call(
        functools.partial(need_kernel, feat_blocks, hid_blocks),
        "needed_features",
        out_shape=ints(2),
        in_specs=[SMEM],
        out_specs=SMEM,
    )(slots)
    rows = jax.ShapeDtypeStruct((4, owners * entries + GROUP), jnp.int32)
    one, two = kernel_call(
        functools.partial(list_kernel, feat_blocks, hid_blocks),
        "list_entries",
        out_shape=[rows] * 2,
        in_specs=[SMEM],
        out_specs=[SMEM] * 2,
    )(slots)
    masks = [mine] + [lax.ppermute(mine, "ch", move) for move in rounds(n)]
    tok = lax.axis_index("tok")
    where = jnp.stack([lax.axis_index("ch"), tok % 2, tok // 2]).astype(jnp.int32)
    fetch_rows = room(FETCH_ROWS, n, 2 * per_slice)
    back_rows = room(BACK_ROWS, n, per_slice)
    meta, levels = kernel_call(
        functools.partial(plan_kernel, n, per_slice, fetch_rows, back_rows),
        "plan",
        out_shape=[ints(META_MASKS + 2 * n), ints(3)],
        in_specs=[SMEM] * (n + 1),
        out_specs=[SMEM] * 2,
    )(where, *masks)
    xs, dys = lax.switch(
        levels[0], [functools.partial(fetch_blocks, row, n, size) for row in fetch_rows], meta, inputs, grad_out
    )
    own, acts, pres, *backs = kernel_call(
        functools.partial(shard_kernel, n, per_slice, hid_blocks),
        "shard_blocks",
        out_shape=[
            floats(tokens, width),
            *[floats(hid_blocks, tokens, size)] * 2,
            *[pltpu.VMEM((per_slice, tokens, size), jnp.float32)] * (n - 1),
        ],
        in_specs=[SMEM] * 3 + [ANY] * 4,
        out_specs=[VMEM] + [ANY] * (n + 1),
        scratch_shapes=[
            pltpu.VMEM((feat_blocks, tokens, size), jnp.float32),
            pltpu.VMEM((feat_blocks, tokens, size), jnp.float32),
            pltpu.VMEM((feat_blocks + 1, tokens, size), jnp.float32),
            pltpu.VMEM((hid_blocks + 1, tokens, size), jnp.float32),
            pltpu.VMEM((hid_blocks + 1, tokens, size), jnp.float32),
            pltpu.VMEM(w_one.shape, jnp.float32),
            pltpu.VMEM(w_two.shape, jnp.float32),
            pltpu.SemaphoreType.DMA((2, feat_blocks)),
            pltpu.SemaphoreType.DMA((feat_blocks,)),
            pltpu.SemaphoreType.DMA((2,)),
            pltpu.SemaphoreType.DMA((2, hid_blocks)),
        ],
        flops=5 * 10**9,
        moved=16 * 2**20,
    )(meta, one, two, xs, dys, *kept_in(pltpu.HBM, w_one, w_two))
    factor = 1.0 / math.sqrt(inputs.shape[0] * lax.axis_size("tok"))
    grad_x, grad_one, grad_two = lax.switch(
        levels[1],
        [functools.partial(send_results, row, n, m, hid_blocks, entries, factor) for row in back_rows],
        levels[2],
        meta,
        one,
        two,
        xs,
        dys,
        acts,
        pres,
        own,
        *backs,
    )
    grad_one = grad_one.reshape(1, 1, entries, size, size)
    grad_two = grad_two.reshape(1, 1, entries, size, size)
    return (grad_x, grad_one, grad_two)


def solution(mesh):
    in_specs = (
        P("tok", "ch"),
        P("tok", "ch"),
        P(None, "ch", None, None, None),
        P(None, "ch", None),
        P(None, "ch", None, None, None),
        P(None, "ch", None),
    )
    out_specs = (P("tok", "ch"), P("tok", "ch", None, None, None), P("tok", "ch", None, None, None))
    return jax.shard_map(body, mesh=mesh, in_specs=in_specs, out_specs=out_specs, check_vma=False)
```
